1024 devices in a mesh: row: 64 (over x_lo, z), col: 16 (over y, x_hi, core).
Axes of the slice: x: 4 (x_hi: 2, x_lo: 2; x = x_hi * 2 + x_lo), y: 4, z: 32, core: 2. Of those that a mesh axis runs over, the one named last changes fastest.
Arguments:
- tiles: bfloat16 [64, 384, 256, 256], P('row', 'col'), may hold values from -0.0546875 to 0.0546875
- tile_slot: int32 [64, 384], P('row', 'col'), may hold values from 0 to 31
- tile_count: int32 [64, 16], P('row', 'col'), may hold values from 1 to 24, 192 in all within a row
- feats: bfloat16 [32768, 256], P('col'), may hold values from -6 to 6
- weight: bfloat16 [256, 256], replicated, may hold values from -0.375 to 0.375
- out_grad: bfloat16 [65536, 256], P(('row', 'col')), may hold values from -6 to 6
Outputs:
- activated: bfloat16 [65536, 256], P(('row', 'col'))
- weight_grad: float32 [256, 256], replicated
- window_grad: bfloat16 [16, 2048, 256], P('col', 'row')
The draws below stay inside these ranges and needn't reach their ends.
Inputs may be any that keep to these rules, and one draw needn't show every extreme that they name: `tile_count`: some block in every draw has all 24 slots in use.
All inputs are finite; a program needn't handle non-finite values.
Results may differ from the reference program's by a relative error of at most 0.0065.
Values may be sent and summed in bfloat16 or wider, within the bound.
No kernel may reach another device: no remote copies, remote signals or barrier semaphores. Data moves between devices by JAX's collectives and lax.ppermute only.
A program may use at most 64 MiB of HBM per device.

```python
import math
import jax
import jax.numpy as jnp
import numpy as np
from jax import lax

F = 256
TILE = 256
TPD = 24
RT = 4
CT = 8
NODES = 65536
WCOLS = 32768
N_ROW = 64
N_COL = 16


def set_ends(result, rng, low, top_value):
    spot = [jax.random.randint(jax.random.fold_in(rng, axis), (), 0, length) for axis, length in enumerate(result.shape)]
    longest = result.shape.index(max(result.shape))
    next_to = spot[:longest] + [(spot[longest] + 1) % result.shape[longest]] + spot[longest + 1:]
    return result.at[tuple(spot)].set(low).at[tuple(next_to)].set(top_value)


def steps_of(stream_key, dims, shards, low, largest):
    gain, own = 1.0, jax.random.fold_in(stream_key, 6)
    for axis_at, parts in shards:
        steps = jnp.exp(jax.random.uniform(jax.random.fold_in(own, axis_at), (parts,), jnp.float32, low / len(shards), largest / len(shards)))
        gain = gain * jnp.repeat(steps, dims[axis_at] // parts).reshape([-1 if axis == axis_at else 1 for axis in range(len(dims))])
    return gain


def length_profile(count, total, limit, lean):
    loads = [(1 << 20) // math.isqrt(grade ** lean) + 1 for grade in range(2, count + 1)]
    surplus, given = total - limit - (count - 1), [1] * (count - 1)
    while surplus > 0:
        movable = [i for i in range(count - 1) if given[i] < limit]
        pool, budget = sum([loads[i] for i in movable]), surplus
        for i in movable:
            more = min(limit - given[i], max(1, budget * loads[i] // pool), surplus)
            given[i] = given[i] + more
            surplus = surplus - more
    return np.array([limit] + given)


def ragged(own_key, number_of, total, most, lean):
    if number_of == 2:
        one = jax.random.randint(own_key, (), max(1, total - most), min(most, total - 1) + 1)
        return jnp.stack([one, total - one])
    tallies = jnp.asarray(length_profile(number_of, total, most, lean), jnp.int32)
    couples = (number_of - 1) // 2
    source_of, sink = tallies[1:1 + 2 * couples:2], tallies[2:2 + 2 * couples:2]
    margin = jnp.minimum(source_of - 1, most - sink)
    moved = jax.random.randint(jax.random.fold_in(own_key, 1), (couples,), 0, 1 << 20) % (margin + 1)
    tallies = tallies.at[1:1 + 2 * couples:2].set(source_of - moved).at[2:2 + 2 * couples:2].set(sink + moved)
    return tallies[jax.random.permutation(jax.random.fold_in(own_key, 2), number_of)]


def centred(stream_key, shape, width, most, split=(), kind=jnp.bfloat16):
    result = width * jax.random.normal(stream_key, shape, jnp.float32)
    if split:
        result = result * steps_of(stream_key, shape, split, -0.22, 0.18)
    return jnp.clip(result, -most, most).astype(kind)


def setup_inputs(seed: int = 0) -> dict:
    seeds = jax.random.split(jax.random.key(seed), 7)
    return {
        "tiles": centred(seeds[0], (N_ROW, N_COL * TPD, TILE, TILE), (TILE * N_COL * TPD // (2 * RT)) ** -0.5, 0.0546875, ((0, 64), (1, 16))),
        "tile_slot": set_ends(jax.random.randint(seeds[1], (N_ROW, N_COL * TPD), 0, RT * CT), jax.random.fold_in(seeds[1], 1), 0, (RT * CT) - 1).astype(jnp.int32),
        "tile_count": jax.vmap(lambda own: ragged(own, N_COL, N_COL * TPD // 2, TPD, 2))(jax.random.split(seeds[2], N_ROW)).reshape((N_ROW, N_COL)).astype(jnp.int32),
        "feats": centred(seeds[3], (WCOLS, F), 1.0, 6.0, ((0, 16),)),
        "weight": centred(seeds[4], (F, F), F ** -0.5, 0.375),
        "out_grad": centred(seeds[5], (NODES, F), 1.0, 6.0, ((0, 1024),)),
    }


def reference(tiles, tile_slot, tile_count, feats, weight, out_grad):
    highest = lax.Precision.HIGHEST
    block_tiles = tiles.reshape(N_ROW, N_COL, TPD, TILE, TILE)
    slot_rows = tile_slot.reshape(N_ROW, N_COL, TPD)
    feature_tiles = feats.reshape(N_COL, CT, TILE, F)
    column_ids = jnp.arange(N_COL)[:, None]

    def forward_row(running, inputs):
        blocks, slots, counts = inputs
        col_index = slots % CT
        row_index = slots // CT
        chosen = feature_tiles[column_ids, col_index]
        products = jnp.einsum("ctij,ctjf->ctif", blocks.astype(jnp.float32), chosen.astype(jnp.float32), precision=highest)
        live_mask = (jnp.arange(TPD)[None, :] < counts[:, None]).astype(jnp.float32)
        onehot = (row_index[..., None] == jnp.arange(RT)).astype(jnp.float32) * live_mask[..., None]
        return running, jnp.einsum("ctk,ctif->kif", onehot, products, precision=highest)

    unused, sums = lax.scan(forward_row, jnp.float32(0.0), (block_tiles, slot_rows, tile_count))
    aggregated = sums.reshape(NODES, F).astype(jnp.bfloat16)
    pre_act = jnp.dot(aggregated, weight, preferred_element_type=jnp.float32)
    sigmoid_pre = jax.nn.sigmoid(pre_act)
    activated = (pre_act * sigmoid_pre).astype(jnp.bfloat16)
    grad_pre = (out_grad.astype(jnp.float32) * sigmoid_pre * (1.0 + pre_act * (1.0 - sigmoid_pre))).astype(jnp.bfloat16)
    weight_grad = lax.dot_general(aggregated, grad_pre, (((0,), (0,)), ((), ())), preferred_element_type=jnp.float32) * (float(NODES) ** -0.5)
    grad_agg = jnp.dot(grad_pre, weight.T, preferred_element_type=jnp.float32).astype(jnp.bfloat16)
    grad_tiles = grad_agg.reshape(N_ROW, RT, TILE, F)

    def backward_row(running, inputs):
        blocks, slots, counts, grads = inputs
        col_index = slots % CT
        row_index = slots // CT
        chosen = grads[row_index]
        products = jnp.einsum("ctij,ctif->ctjf", blocks.astype(jnp.float32), chosen.astype(jnp.float32), precision=highest)
        live_mask = (jnp.arange(TPD)[None, :] < counts[:, None]).astype(jnp.float32)
        onehot = (col_index[..., None] == jnp.arange(CT)).astype(jnp.float32) * live_mask[..., None]
        return running + jnp.einsum("ctk,ctjf->ckjf", onehot, products, precision=highest), jnp.float32(0.0)

    start = jnp.zeros((N_COL, CT, TILE, F), jnp.float32)
    window_sum, unused_two = lax.scan(backward_row, start, (block_tiles, slot_rows, tile_count, grad_tiles))
    window_grad = window_sum.reshape(N_COL, CT * TILE, F).astype(jnp.bfloat16)
    return activated, weight_grad, window_grad
```

```python
import functools
import math

import jax
import jax.numpy as jnp
from jax import lax
from jax.experimental import pallas as pl
from jax.experimental.pallas import tpu as pltpu
from jax.sharding import Mesh
from jax.sharding import PartitionSpec as P

RT, CT, TPD, TILE, F = 4, 8, 24, 256, 256
N_ROW, N_COL = 64, 16
SHARE = RT * TILE // N_COL
WIN = CT * TILE // N_ROW
WG = F // N_COL

AXES = ("xl", "z16", "z8", "z4", "z2", "z1", "y2", "y1", "xh", "c")
ROW, COL = AXES[:6], AXES[6:]
CHIPS = COL[:3]
NEAR, FAR = ("xl", "z2", "z1"), ("z16", "z8", "z4")
PARTS = 8

BF, F32 = jnp.bfloat16, jnp.float32
SMEM = pl.BlockSpec(memory_space=pltpu.SMEM)
VMEM = pl.BlockSpec(memory_space=pltpu.VMEM)
ANY = pl.BlockSpec(memory_space=pl.ANY)
LIMIT = pltpu.CompilerParams(vmem_limit_bytes=40 << 20)


def fetch(tiles_ref, buf, sems, t):
    return pltpu.make_async_copy(tiles_ref.at[0, t], buf.at[t], sems.at[t])


def fetch_all(n, tiles_ref, buf, sems):
    def begin(t, carry):
        fetch(tiles_ref, buf, sems, t).start()
        return carry

    lax.fori_loop(0, n, begin, 0)


def forward_kernel(slot_ref, count_ref, tiles_ref, feats_ref, out_ref, buf, acc, sems):
    n = count_ref[0]
    fetch_all(n, tiles_ref, buf, sems)
    acc[...] = jnp.zeros_like(acc)

    def step(t, carry):
        fetch(tiles_ref, buf, sems, t).wait()
        slot = slot_ref[t]
        source = feats_ref[pl.ds(pl.multiple_of((slot % CT) * TILE, TILE), TILE), :]
        acc[slot // CT] += jnp.dot(buf[t], source, preferred_element_type=F32)
        return carry

    lax.fori_loop(0, n, step, 0)
    out_ref[...] = acc[...].reshape(RT * TILE, F).astype(BF)


def middle_kernel(parts_ref, weight_ref, out_grad_ref, act_ref, send_ref):
    total = parts_ref[0].astype(F32)
    for j in range(1, N_COL):
        total += parts_ref[j].astype(F32)
    agg = total.astype(BF)
    weight = weight_ref[...]
    pre = jnp.dot(agg, weight, preferred_element_type=F32)
    sig = jax.nn.sigmoid(pre)
    act_ref[...] = (pre * sig).astype(BF)
    grad_pre = (out_grad_ref[...].astype(F32) * sig * (1.0 + pre * (1.0 - sig))).astype(BF)
    share = lax.dot_general(
        grad_pre, weight, (((1,), (1,)), ((), ())), preferred_element_type=F32
    ).astype(BF)
    local = lax.dot_general(
        agg, grad_pre, (((0,), (0,)), ((), ())), preferred_element_type=F32
    ).astype(BF)
    for j in range(PARTS):
        send_ref[j, 0:SHARE] = share
        send_ref[j, SHARE : SHARE + 2 * WG] = local[2 * j * WG : 2 * (j + 1) * WG]


def put_pair(ref, start, value):
    high = value.astype(BF)
    low = (value - high.astype(F32)).astype(BF)
    for p in range(PARTS):
        ref[p, start : start + WG] = high
        ref[p, start + WG : start + 2 * WG] = low


def total_of(parts_ref, start, size):
    total = parts_ref[0, pl.ds(start, size)].astype(F32)
    for p in range(1, PARTS):
        total += parts_ref[p, pl.ds(start, size)].astype(F32)
    return total


def pair_total(parts_ref, start):
    return total_of(parts_ref, start, WG) + total_of(parts_ref, start + WG, WG)


def backward_kernel(
    slot_ref, count_ref, core_ref, tiles_ref, own_ref, other_ref, send_ref,
    buf, grads, acc, sems,
):
    n, core = count_ref[0], core_ref[0]
    fetch_all(n, tiles_ref, buf, sems)
    acc[...] = jnp.zeros_like(acc)
    for j in range(PARTS):
        k, at = divmod(2 * j * SHARE, TILE)
        for ref, c in ((own_ref, core), (other_ref, 1 - core)):
            place = pl.multiple_of(at + c * SHARE, SHARE)
            grads[k, pl.ds(place, SHARE)] = ref[j, 0:SHARE]
    half = pl.multiple_of(SHARE + core * WG, WG)
    wgrad = total_of(own_ref, half, WG) + total_of(other_ref, half, WG)

    def step(t, carry):
        fetch(tiles_ref, buf, sems, t).wait()
        slot = slot_ref[t]
        acc[slot % CT] += lax.dot_general(
            buf[t], grads[slot // CT], (((0,), (0,)), ((), ())), preferred_element_type=F32
        )
        return carry

    lax.fori_loop(0, n, step, 0)
    for k in range(N_ROW):
        part, place = (k >> 5) * 4 + (k & 3), (k >> 2) & 7
        tile, at = divmod(k * WIN, TILE)
        send_ref[part, place * WIN : (place + 1) * WIN] = acc[tile, at : at + WIN].astype(BF)
    put_pair(send_ref, PARTS * WIN, wgrad)


def merge_kernel(parts_ref, send_ref):
    for q in range(PARTS):
        send_ref[q, 0:WIN] = total_of(parts_ref, q * WIN, WIN).astype(BF)
    put_pair(send_ref, WIN, pair_total(parts_ref, PARTS * WIN))


def last_kernel(scale, parts_ref, win_ref, wgrad_ref):
    win_ref[0] = total_of(parts_ref, 0, WIN).astype(BF)
    wgrad = pair_total(parts_ref, WIN) * scale
    for j in range(N_COL):
        wgrad_ref[j] = wgrad


def exchange(parts, axes):
    return lax.all_to_all(parts, axes, 0, 0, tiled=True)


def shape(*dims, dtype=BF):
    return jax.ShapeDtypeStruct(dims, dtype)


def on_device(tiles, tile_slot, tile_count, feats, weight, out_grad):
    slots, count = tile_slot.reshape(TPD), tile_count.reshape(1)
    tile_buf = pltpu.VMEM((TPD, TILE, TILE), BF)
    sems = pltpu.SemaphoreType.DMA((TPD,))

    row_partial = pl.pallas_call(
        forward_kernel,
        out_shape=shape(RT * TILE, F),
        in_specs=[SMEM, SMEM, ANY, VMEM],
        out_specs=VMEM,
        scratch_shapes=[tile_buf, pltpu.VMEM((RT, TILE, F), F32), sems],
        compiler_params=LIMIT,
    )(slots, count, tiles, feats)
    row_parts = exchange(row_partial.reshape(N_COL, SHARE, F), COL)

    activated, grad_send = pl.pallas_call(
        middle_kernel,
        out_shape=(shape(SHARE, F), shape(PARTS, SHARE + 2 * WG, F)),
        in_specs=[VMEM] * 3,
        out_specs=(VMEM, VMEM),
        compiler_params=LIMIT,
    )(row_parts, weight, out_grad)
    own_parts = exchange(grad_send, CHIPS)
    other_parts = lax.ppermute(own_parts, "c", [(0, 1), (1, 0)])

    send_near = pl.pallas_call(
        backward_kernel,
        out_shape=shape(PARTS, PARTS * WIN + 2 * WG, F),
        in_specs=[SMEM, SMEM, SMEM, ANY, VMEM, VMEM],
        out_specs=VMEM,
        scratch_shapes=[
            tile_buf,
            pltpu.VMEM((RT, TILE, F), BF),
            pltpu.VMEM((CT, TILE, F), F32),
            sems,
        ],
        compiler_params=LIMIT,
    )(slots, count, lax.axis_index("c").reshape(1), tiles, own_parts, other_parts)
    near_parts = exchange(send_near, NEAR)

    send_far = pl.pallas_call(
        merge_kernel,
        out_shape=shape(PARTS, WIN + 2 * WG, F),
        in_specs=[VMEM],
        out_specs=VMEM,
        compiler_params=LIMIT,
    )(near_parts)
    far_parts = exchange(send_far, FAR)

    window_grad, wgrad_send = pl.pallas_call(
        functools.partial(last_kernel, 1.0 / math.sqrt(RT * TILE * N_ROW)),
        out_shape=(shape(1, WIN, F), shape(N_COL, WG, F, dtype=F32)),
        in_specs=[VMEM],
        out_specs=(VMEM, VMEM),
        compiler_params=LIMIT,
    )(far_parts)
    weight_grad = exchange(wgrad_send, COL).reshape(F, F)
    return (activated, weight_grad, window_grad)


def solution(mesh):
    fine = Mesh(mesh.devices.reshape((2,) * len(AXES)), AXES)
    placed = (
        P(ROW, COL, None, None),
        P(ROW, COL),
        P(ROW, COL),
        P(COL, None),
        P(),
        P(AXES, None),
    )
    return jax.shard_map(
        on_device,
        mesh=fine,
        in_specs=placed,
        out_specs=(P(AXES, None), P(), P(COL, ROW, None)),
        check_vma=False,
    )
```

```python
import functools
import math

import jax
import jax.numpy as jnp
from jax import lax
from jax.experimental import pallas as pl
from jax.experimental.pallas import tpu as pltpu
from jax.sharding import Mesh
from jax.sharding import PartitionSpec as P

RT, CT, TPD, TILE, F = 4, 8, 24, 256, 256
N_ROW, N_COL = 64, 16
SHARE = RT * TILE // N_COL
WIN = CT * TILE // N_ROW
WG = F // N_COL

AXES = ("xl", "z16", "z8", "z4", "z2", "z1", "y2", "y1", "xh", "c")
ROW, COL = AXES[:6], AXES[6:]
CHIPS = COL[:3]
NEAR, FAR = ("xl", "z1"), ("z16", "z8", "z4")
N_CHIP, N_NEAR, N_FAR = 8, 4, 8
HALF = N_FAR * WIN

BF, F32 = jnp.bfloat16, jnp.float32
SMEM = pl.BlockSpec(memory_space=pltpu.SMEM)
VMEM = pl.BlockSpec(memory_space=pltpu.VMEM)
HBM = pl.BlockSpec(memory_space=pltpu.MemorySpace.HBM)
LIMIT = pltpu.CompilerParams(vmem_limit_bytes=40 << 20)
ALL_VMEM = pltpu.CompilerParams(vmem_limit_bytes=59 << 20)


FETCH = 12
GROUP = 8


def forward_kernel(
    slot_hbm, count_hbm, tiles_hbm, feats_hbm, out_ref,
    slot_ref, count_ref, buf, feats, acc, tile_sems, sems,
):
    def tile_copy(g):
        rows = pl.ds(g * FETCH, FETCH)
        return pltpu.make_async_copy(tiles_hbm.at[0, rows], buf.at[rows], tile_sems.at[g])

    small = [
        pltpu.make_async_copy(slot_hbm, slot_ref, sems.at[0]),
        pltpu.make_async_copy(count_hbm, count_ref, sems.at[1]),
        pltpu.make_async_copy(feats_hbm, feats, sems.at[2]),
    ]
    for copy in small:
        copy.start()
    for g in range(TPD // FETCH):
        tile_copy(g).start()
    acc[...] = jnp.zeros_like(acc)
    for copy in small:
        copy.wait()
    n = count_ref[0, 0]

    def multiply(first):
        products = []
        for u in range(4):
            t = first + u
            slot = slot_ref[0, t]
            source = feats[pl.ds(pl.multiple_of((slot & 7) * TILE, TILE), TILE), :]
            product = jnp.dot(buf[t], source, preferred_element_type=F32)
            products.append((slot >> 3, jnp.where(t < n, product, 0.0)))
        for row, product in products:
            acc[row] += product

    for g in range(TPD // FETCH):
        tile_copy(g).wait()
        for first in range(g * FETCH, (g + 1) * FETCH, 4):

            @pl.when(first < n)
            def _(first=first):
                multiply(first)

    out_ref[...] = acc[...].reshape(RT * TILE, F).astype(BF)


def middle_kernel(parts_ref, weight_ref, out_grad_ref, act_ref, send_ref):
    total = parts_ref[0].astype(F32)
    for j in range(1, N_COL):
        total += parts_ref[j].astype(F32)
    agg = total.astype(BF)
    weight = weight_ref[...]
    pre = jnp.dot(agg, weight, preferred_element_type=F32)
    sig = jax.nn.sigmoid(pre)
    act_ref[...] = (pre * sig).astype(BF)
    grad_pre = (out_grad_ref[...].astype(F32) * sig * (1.0 + pre * (1.0 - sig))).astype(BF)
    share = lax.dot_general(
        grad_pre, weight, (((1,), (1,)), ((), ())), preferred_element_type=F32
    ).astype(BF)
    local = lax.dot_general(
        agg, grad_pre, (((0,), (0,)), ((), ())), preferred_element_type=F32
    ).astype(BF)
    for j in range(N_CHIP):
        send_ref[j, 0:SHARE] = share
        send_ref[j, SHARE : SHARE + 2 * WG] = local[2 * j * WG : 2 * (j + 1) * WG]


def total_of(parts_ref, start, size):
    total = parts_ref[0, pl.ds(start, size)].astype(F32)
    for p in range(1, parts_ref.shape[0]):
        total += parts_ref[p, pl.ds(start, size)].astype(F32)
    return total


def backward_kernel(
    slot_ref, count_ref, core_ref, tiles_ref, own_ref, other_ref, send_ref, grads, acc
):
    n, core = count_ref[0, 0], core_ref[0]
    acc[...] = jnp.zeros_like(acc)
    for j in range(N_CHIP):
        k, at = divmod(2 * j * SHARE, TILE)
        for ref, c in ((own_ref, core), (other_ref, 1 - core)):
            place = pl.multiple_of(at + c * SHARE, SHARE)
            grads[k, pl.ds(place, SHARE)] = ref[j, 0:SHARE]
    half = pl.multiple_of(SHARE + core * WG, WG)
    wgrad = (total_of(own_ref, half, WG) + total_of(other_ref, half, WG)).astype(BF)
    for p in range(N_NEAR):
        send_ref[p, 2 * HALF : 2 * HALF + WG] = wgrad

    def step(g, carry):
        products = []
        for u in range(GROUP):
            t = g * GROUP + u
            slot = slot_ref[0, t]
            product = lax.dot_general(
                tiles_ref[0, t],
                grads[slot >> 3],
                (((0,), (0,)), ((), ())),
                preferred_element_type=F32,
            )
            products.append((slot & 7, jnp.where(t < n, product, 0.0)))
        for col, product in products:
            acc[col] += product
        return carry

    lax.fori_loop(0, (n + GROUP - 1) // GROUP, step, 0)
    for k in range(N_ROW):
        part, place = (k >> 5) * 2 + (k & 1), (k >> 1) & 15
        tile, at = divmod(k * WIN, TILE)
        send_ref[part, place * WIN : (place + 1) * WIN] = acc[tile, at : at + WIN].astype(BF)


def halve_kernel(z2_ref, parts_ref, keep_ref, send_ref):
    z2 = z2_ref[0]
    for f in range(N_FAR):
        rows = slice(f * WIN, (f + 1) * WIN)
        kept = pl.multiple_of((2 * f + z2) * WIN, WIN)
        sent = pl.multiple_of((2 * f + 1 - z2) * WIN, WIN)
        keep_ref[rows] = total_of(parts_ref, kept, WIN)
        send_ref[rows] = total_of(parts_ref, sent, WIN).astype(BF)
    send_ref[HALF : HALF + WG] = total_of(parts_ref, 2 * HALF, WG).astype(BF)


def deal_kernel(keep_ref, sent_ref, came_ref, send_ref):
    wrows = slice(HALF, HALF + WG)
    wgrad = (sent_ref[wrows].astype(F32) + came_ref[wrows].astype(F32)).astype(BF)
    for f in range(N_FAR):
        rows = slice(f * WIN, (f + 1) * WIN)
        send_ref[f, 0:WIN] = (keep_ref[rows] + came_ref[rows].astype(F32)).astype(BF)
        send_ref[f, WIN : WIN + WG] = wgrad


def last_kernel(scale, parts_ref, win_ref, wgrad_ref):
    win_ref[0] = total_of(parts_ref, 0, WIN).astype(BF)
    wgrad = total_of(parts_ref, WIN, WG) * scale
    for j in range(N_COL):
        wgrad_ref[j] = wgrad


def exchange(parts, axes):
    return lax.all_to_all(parts, axes, 0, 0, tiled=True)


def shape(*dims, dtype=BF):
    return jax.ShapeDtypeStruct(dims, dtype)


def position(axis):
    return lax.axis_index(axis).astype(jnp.int32).reshape(1)


def on_device(tiles, tile_slot, tile_count, feats, weight, out_grad):
    swap = [(0, 1), (1, 0)]
    row_partial = pl.pallas_call(
        forward_kernel,
        out_shape=shape(RT * TILE, F),
        in_specs=[HBM] * 4,
        out_specs=VMEM,
        scratch_shapes=[
            pltpu.SMEM((1, TPD), jnp.int32),
            pltpu.SMEM((1, 1), jnp.int32),
            pltpu.VMEM((TPD, TILE, TILE), BF),
            pltpu.VMEM((CT * TILE, F), BF),
            pltpu.VMEM((RT, TILE, F), F32),
            pltpu.SemaphoreType.DMA((TPD // FETCH,)),
            pltpu.SemaphoreType.DMA((3,)),
        ],
        compiler_params=ALL_VMEM,
    )(tile_slot, tile_count, tiles, feats)
    row_parts = exchange(row_partial.reshape(N_COL, SHARE, F), COL)

    activated, grad_send = pl.pallas_call(
        middle_kernel,
        out_shape=(shape(SHARE, F), shape(N_CHIP, SHARE + 2 * WG, F)),
        in_specs=[VMEM] * 3,
        out_specs=(VMEM, VMEM),
        compiler_params=LIMIT,
    )(row_parts, weight, out_grad)
    own_parts = exchange(grad_send, CHIPS)
    other_parts = lax.ppermute(own_parts, "c", swap)

    near_send = pl.pallas_call(
        backward_kernel,
        out_shape=shape(N_NEAR, 2 * HALF + WG, F),
        in_specs=[SMEM] * 3 + [VMEM] * 3,
        out_specs=VMEM,
        scratch_shapes=[
            pltpu.VMEM((RT, TILE, F), BF),
            pltpu.VMEM((CT, TILE, F), F32),
        ],
        compiler_params=LIMIT,
    )(tile_slot, tile_count, position("c"), tiles, own_parts, other_parts)
    near_parts = exchange(near_send, NEAR)

    kept, half_send = pl.pallas_call(
        halve_kernel,
        out_shape=(shape(HALF, F, dtype=F32), shape(HALF + WG, F)),
        in_specs=[SMEM, VMEM],
        out_specs=(VMEM, VMEM),
        compiler_params=LIMIT,
    )(position("z2"), near_parts)
    half_came = lax.ppermute(half_send, "z2", swap)

    far_send = pl.pallas_call(
        deal_kernel,
        out_shape=shape(N_FAR, WIN + WG, F),
        in_specs=[VMEM] * 3,
        out_specs=VMEM,
        compiler_params=LIMIT,
    )(kept, half_send, half_came)
    far_parts = exchange(far_send, FAR)

    window_grad, wgrad_send = pl.pallas_call(
        functools.partial(last_kernel, 1.0 / math.sqrt(RT * TILE * N_ROW)),
        out_shape=(shape(1, WIN, F), shape(N_COL, WG, F, dtype=F32)),
        in_specs=[VMEM],
        out_specs=(VMEM, VMEM),
        compiler_params=LIMIT,
    )(far_parts)
    weight_grad = exchange(wgrad_send, COL).reshape(F, F)
    return (activated, weight_grad, window_grad)


def solution(mesh):
    fine = Mesh(mesh.devices.reshape((2,) * len(AXES)), AXES)
    placed = (
        P(ROW, COL, None, None),
        P(ROW, COL),
        P(ROW, COL),
        P(COL, None),
        P(),
        P(AXES, None),
    )
    return jax.shard_map(
        on_device,
        mesh=fine,
        in_specs=placed,
        out_specs=(P(AXES, None), P(), P(COL, ROW, None)),
        check_vma=False,
    )
```

```python
import functools
import math

import jax
import jax.numpy as jnp
from jax import lax
from jax.experimental import pallas as pl
from jax.experimental.pallas import tpu as pltpu
from jax.sharding import Mesh
from jax.sharding import PartitionSpec as P

RT, CT, TPD, TILE, F = 4, 8, 24, 256, 256
N_ROW, N_COL = 64, 16
SHARE = RT * TILE // N_COL
WIN = CT * TILE // N_ROW
WG = F // N_COL

AXES = ("xl", "z16", "z8", "z4", "z2", "z1", "y2", "y1", "xh", "c")
ROW, COL = AXES[:6], AXES[6:]
CHIPS = COL[:3]
NEAR, FAR = ("xl", "z1"), ("z16", "z8", "z4")
N_CHIP, N_NEAR, N_FAR = 8, 4, 8
HALF = N_FAR * WIN

BF, F32 = jnp.bfloat16, jnp.float32
SMEM = pl.BlockSpec(memory_space=pltpu.SMEM)
VMEM = pl.BlockSpec(memory_space=pltpu.VMEM)
HBM = pl.BlockSpec(memory_space=pltpu.MemorySpace.HBM)
LIMIT = pltpu.CompilerParams(vmem_limit_bytes=16 << 20)
ALL_VMEM = pltpu.CompilerParams(vmem_limit_bytes=59 << 20)


FETCHES = ((0, 4), (4, 12), (12, 24))
GROUP = 8


def forward_kernel(
    slot_hbm, count_hbm, tiles_hbm, feats_hbm, out_ref,
    slot_ref, count_ref, buf, feats, acc, tile_sems, sems,
):
    def tile_copy(g):
        first, end = FETCHES[g]
        rows = pl.ds(first, end - first)
        return pltpu.make_async_copy(tiles_hbm.at[0, rows], buf.at[rows], tile_sems.at[g])

    small = [
        pltpu.make_async_copy(slot_hbm, slot_ref, sems.at[0]),
        pltpu.make_async_copy(count_hbm, count_ref, sems.at[1]),
        pltpu.make_async_copy(feats_hbm, feats, sems.at[2]),
    ]
    for copy in small:
        copy.start()
    for g in range(len(FETCHES)):
        tile_copy(g).start()
    acc[...] = jnp.zeros_like(acc)
    for copy in small:
        copy.wait()
    n = count_ref[0, 0]

    def multiply(first):
        products = []
        for u in range(4):
            t = first + u
            slot = slot_ref[0, t]
            source = feats[pl.ds(pl.multiple_of((slot & 7) * TILE, TILE), TILE), :]
            product = jnp.dot(buf[t], source, preferred_element_type=F32)
            products.append((slot >> 3, jnp.where(t < n, product, 0.0)))
        for row, product in products:
            acc[row] += product

    for g in range(len(FETCHES)):
        tile_copy(g).wait()
        for first in range(*FETCHES[g], 4):

            @pl.when(first < n)
            def _(first=first):
                multiply(first)

    out_ref[...] = acc[...].reshape(RT * TILE, F).astype(BF)


def middle_kernel(parts_ref, weight_ref, out_grad_ref, act_ref, send_ref):
    total = parts_ref[0].astype(F32)
    for j in range(1, N_COL):
        total += parts_ref[j].astype(F32)
    agg = total.astype(BF)
    weight = weight_ref[...]
    pre = jnp.dot(agg, weight, preferred_element_type=F32)
    sig = jax.nn.sigmoid(pre)
    act_ref[...] = (pre * sig).astype(BF)
    grad_pre = (out_grad_ref[...].astype(F32) * sig * (1.0 + pre * (1.0 - sig))).astype(BF)
    share = lax.dot_general(
        grad_pre, weight, (((1,), (1,)), ((), ())), preferred_element_type=F32
    ).astype(BF)
    local = lax.dot_general(
        agg, grad_pre, (((0,), (0,)), ((), ())), preferred_element_type=F32
    ).astype(BF)
    for j in range(N_CHIP):
        send_ref[j, 0:SHARE] = share
        send_ref[j, SHARE : SHARE + 2 * WG] = local[2 * j * WG : 2 * (j + 1) * WG]


def total_of(parts_ref, start, size):
    total = parts_ref[0, pl.ds(start, size)].astype(F32)
    for p in range(1, parts_ref.shape[0]):
        total += parts_ref[p, pl.ds(start, size)].astype(F32)
    return total


def backward_kernel(
    slot_ref, count_ref, place_ref, tiles_ref, own_ref, other_ref, send_ref, grads, acc
):
    n, core = count_ref[0, 0], place_ref[0]
    acc[...] = jnp.zeros_like(acc)
    for j in range(N_CHIP):
        k, at = divmod(2 * j * SHARE, TILE)
        for ref, c in ((own_ref, core), (other_ref, 1 - core)):
            place = pl.multiple_of(at + c * SHARE, SHARE)
            grads[k, pl.ds(place, SHARE)] = ref[j, 0:SHARE]
    half = pl.multiple_of(SHARE + core * WG, WG)
    wgrad = (total_of(own_ref, half, WG) + total_of(other_ref, half, WG)).astype(BF)
    for p in range(N_NEAR):
        send_ref[p, 2 * HALF : 2 * HALF + WG] = wgrad

    def step(g, carry):
        products = []
        for u in range(GROUP):
            t = g * GROUP + u
            slot = slot_ref[0, t]
            product = lax.dot_general(
                tiles_ref[0, t],
                grads[slot >> 3],
                (((0,), (0,)), ((), ())),
                preferred_element_type=F32,
            )
            products.append((slot & 7, jnp.where(t < n, product, 0.0)))
        for col, product in products:
            acc[col] += product
        return carry

    lax.fori_loop(0, (n + GROUP - 1) // GROUP, step, 0)
    for k in range(N_ROW):
        part, place = (k >> 5) * 2 + (k & 1), (k >> 1) & 15
        tile, at = divmod(k * WIN, TILE)
        send_ref[part, place * WIN : (place + 1) * WIN] = acc[tile, at : at + WIN].astype(BF)


def halve_kernel(place_ref, parts_ref, keep_ref, send_ref):
    z2 = place_ref[1]
    for f in range(N_FAR):
        rows = slice(f * WIN, (f + 1) * WIN)
        kept = pl.multiple_of((2 * f + z2) * WIN, WIN)
        sent = pl.multiple_of((2 * f + 1 - z2) * WIN, WIN)
        keep_ref[rows] = total_of(parts_ref, kept, WIN)
        send_ref[rows] = total_of(parts_ref, sent, WIN).astype(BF)
    send_ref[HALF : HALF + WG] = total_of(parts_ref, 2 * HALF, WG).astype(BF)


def deal_kernel(keep_ref, sent_ref, came_ref, send_ref):
    wrows = slice(HALF, HALF + WG)
    wgrad = (sent_ref[wrows].astype(F32) + came_ref[wrows].astype(F32)).astype(BF)
    for f in range(N_FAR):
        rows = slice(f * WIN, (f + 1) * WIN)
        send_ref[f, 0:WIN] = (keep_ref[rows] + came_ref[rows].astype(F32)).astype(BF)
        send_ref[f, WIN : WIN + WG] = wgrad


def last_kernel(parts_ref, win_ref, wgrad_ref):
    win_ref[0] = total_of(parts_ref, 0, WIN).astype(BF)
    wgrad = total_of(parts_ref, WIN, WG).astype(BF)
    for j in range(N_COL):
        wgrad_ref[j] = wgrad


def scale_kernel(scale, wgrad_ref, out_ref):
    out_ref[...] = wgrad_ref[...].astype(F32).reshape(F, F) * scale


def exchange(parts, axes):
    return lax.all_to_all(parts, axes, 0, 0, tiled=True)


def shape(*dims, dtype=BF):
    return jax.ShapeDtypeStruct(dims, dtype)


def on_device(tiles, tile_slot, tile_count, feats, weight, out_grad):
    swap = [(0, 1), (1, 0)]
    place = jnp.stack([lax.axis_index("c"), lax.axis_index("z2")]).astype(jnp.int32)
    row_partial = pl.pallas_call(
        forward_kernel,
        out_shape=shape(RT * TILE, F),
        in_specs=[HBM] * 4,
        out_specs=VMEM,
        scratch_shapes=[
            pltpu.SMEM((1, TPD), jnp.int32),
            pltpu.SMEM((1, 1), jnp.int32),
            pltpu.VMEM((TPD, TILE, TILE), BF),
            pltpu.VMEM((CT * TILE, F), BF),
            pltpu.VMEM((RT, TILE, F), F32),
            pltpu.SemaphoreType.DMA((len(FETCHES),)),
            pltpu.SemaphoreType.DMA((3,)),
        ],
        compiler_params=ALL_VMEM,
    )(tile_slot, tile_count, tiles, feats)
    row_parts = exchange(row_partial.reshape(N_COL, SHARE, F), COL)

    activated, grad_send = pl.pallas_call(
        middle_kernel,
        out_shape=(shape(SHARE, F), shape(N_CHIP, SHARE + 2 * WG, F)),
        in_specs=[VMEM] * 3,
        out_specs=(VMEM, VMEM),
        compiler_params=LIMIT,
    )(row_parts, weight, out_grad)
    own_parts = exchange(grad_send, CHIPS)
    other_parts = lax.ppermute(own_parts, "c", swap)

    near_send = pl.pallas_call(
        backward_kernel,
        out_shape=shape(N_NEAR, 2 * HALF + WG, F),
        in_specs=[SMEM] * 3 + [VMEM] * 3,
        out_specs=VMEM,
        scratch_shapes=[
            pltpu.VMEM((RT, TILE, F), BF),
            pltpu.VMEM((CT, TILE, F), F32),
        ],
        compiler_params=LIMIT,
    )(tile_slot, tile_count, place, tiles, own_parts, other_parts)
    near_parts = exchange(near_send, NEAR)

    kept, half_send = pl.pallas_call(
        halve_kernel,
        out_shape=(shape(HALF, F, dtype=F32), shape(HALF + WG, F)),
        in_specs=[SMEM, VMEM],
        out_specs=(VMEM, VMEM),
        compiler_params=LIMIT,
    )(place, near_parts)
    half_came = lax.ppermute(half_send, "z2", swap)

    far_send = pl.pallas_call(
        deal_kernel,
        out_shape=shape(N_FAR, WIN + WG, F),
        in_specs=[VMEM] * 3,
        out_specs=VMEM,
        compiler_params=LIMIT,
    )(kept, half_send, half_came)
    far_parts = exchange(far_send, FAR)

    window_grad, wgrad_send = pl.pallas_call(
        last_kernel,
        out_shape=(shape(1, WIN, F), shape(N_COL, WG, F)),
        in_specs=[VMEM],
        out_specs=(VMEM, VMEM),
        compiler_params=LIMIT,
    )(far_parts)
    wgrad_parts = exchange(wgrad_send, COL)
    weight_grad = pl.pallas_call(
        functools.partial(scale_kernel, 1.0 / math.sqrt(RT * TILE * N_ROW)),
        out_shape=shape(F, F, dtype=F32),
        in_specs=[VMEM],
        out_specs=VMEM,
        compiler_params=LIMIT,
    )(wgrad_parts)
    return (activated, weight_grad, window_grad)


def solution(mesh):
    fine = Mesh(mesh.devices.reshape((2,) * len(AXES)), AXES)
    placed = (
        P(ROW, COL, None, None),
        P(ROW, COL),
        P(ROW, COL),
        P(COL, None),
        P(),
        P(AXES, None),
    )
    return jax.shard_map(
        on_device,
        mesh=fine,
        in_specs=placed,
        out_specs=(P(AXES, None), P(), P(COL, ROW, None)),
        check_vma=False,
    )
```

```python
import functools
import math

import jax
import jax.numpy as jnp
from jax import lax
from jax.experimental import pallas as pl
from jax.experimental.pallas import tpu as pltpu
from jax.sharding import Mesh
from jax.sharding import PartitionSpec as P

RT, CT, TPD, TILE, F = 4, 8, 24, 256, 256
N_ROW, N_COL = 64, 16
SHARE = RT * TILE // N_COL
WIN = CT * TILE // N_ROW
WG = F // N_COL

AXES = ("xl", "z16", "z8", "z4", "z2", "z1", "y2", "y1", "xh", "c")
ROW, COL = AXES[:6], AXES[6:]
CHIPS = COL[:3]
NEAR = ("xl", "z1")
N_CHIP, N_NEAR, N_FAR = 8, 4, 8
FAR_GROUPS = [
    [xl * 32 + f * 4 + (side ^ (f >> 2)) * 2 + z1 for f in range(N_FAR)]
    for xl in range(2)
    for side in range(2)
    for z1 in range(2)
]
HALF = N_FAR * WIN

BF, F32 = jnp.bfloat16, jnp.float32
SMEM = pl.BlockSpec(memory_space=pltpu.SMEM)
VMEM = pl.BlockSpec(memory_space=pltpu.VMEM)
HBM = pl.BlockSpec(memory_space=pltpu.MemorySpace.HBM)
LIMIT = pltpu.CompilerParams(vmem_limit_bytes=16 << 20)
ALL_VMEM = pltpu.CompilerParams(vmem_limit_bytes=59 << 20)


FETCHES = ((0, 4), (4, 12), (12, 24))
GROUP = 8


def forward_kernel(
    slot_hbm, count_hbm, tiles_hbm, feats_hbm, out_ref,
    slot_ref, count_ref, buf, feats, acc, tile_sems, sems,
):
    def tile_copy(g):
        first, end = FETCHES[g]
        rows = pl.ds(first, end - first)
        return pltpu.make_async_copy(tiles_hbm.at[0, rows], buf.at[rows], tile_sems.at[g])

    small = [
        pltpu.make_async_copy(slot_hbm, slot_ref, sems.at[0]),
        pltpu.make_async_copy(count_hbm, count_ref, sems.at[1]),
        pltpu.make_async_copy(feats_hbm, feats, sems.at[2]),
    ]
    for copy in small:
        copy.start()
    for g in range(len(FETCHES)):
        tile_copy(g).start()
    acc[...] = jnp.zeros_like(acc)
    for copy in small:
        copy.wait()
    n = count_ref[0, 0]

    def multiply(first):
        products = []
        for u in range(4):
            t = first + u
            slot = slot_ref[0, t]
            source = feats[pl.ds(pl.multiple_of((slot & 7) * TILE, TILE), TILE), :]
            product = jnp.dot(buf[t], source, preferred_element_type=F32)
            products.append((slot >> 3, jnp.where(t < n, product, 0.0)))
        for row, product in products:
            acc[row] += product

    for g in range(len(FETCHES)):
        tile_copy(g).wait()
        for first in range(*FETCHES[g], 4):

            @pl.when(first < n)
            def _(first=first):
                multiply(first)

    out_ref[...] = acc[...].reshape(RT * TILE, F).astype(BF)


def middle_kernel(parts_ref, weight_ref, out_grad_ref, act_ref, send_ref):
    total = parts_ref[0].astype(F32)
    for j in range(1, N_COL):
        total += parts_ref[j].astype(F32)
    agg = total.astype(BF)
    weight = weight_ref[...]
    pre = jnp.dot(agg, weight, preferred_element_type=F32)
    sig = jax.nn.sigmoid(pre)
    act_ref[...] = (pre * sig).astype(BF)
    grad_pre = (out_grad_ref[...].astype(F32) * sig * (1.0 + pre * (1.0 - sig))).astype(BF)
    share = lax.dot_general(
        grad_pre, weight, (((1,), (1,)), ((), ())), preferred_element_type=F32
    ).astype(BF)
    local = lax.dot_general(
        agg, grad_pre, (((0,), (0,)), ((), ())), preferred_element_type=F32
    ).astype(BF)
    for j in range(N_CHIP):
        send_ref[j, 0:SHARE] = share
        send_ref[j, SHARE : SHARE + 2 * WG] = local[2 * j * WG : 2 * (j + 1) * WG]


def total_of(parts_ref, start, size):
    total = parts_ref[0, pl.ds(start, size)].astype(F32)
    for p in range(1, parts_ref.shape[0]):
        total += parts_ref[p, pl.ds(start, size)].astype(F32)
    return total


def backward_kernel(
    slot_ref, count_ref, place_ref, tiles_ref, own_ref, other_ref, send_ref, grads, acc
):
    n, core = count_ref[0, 0], place_ref[0]
    acc[...] = jnp.zeros_like(acc)
    for j in range(N_CHIP):
        k, at = divmod(2 * j * SHARE, TILE)
        for ref, c in ((own_ref, core), (other_ref, 1 - core)):
            place = pl.multiple_of(at + c * SHARE, SHARE)
            grads[k, pl.ds(place, SHARE)] = ref[j, 0:SHARE]
    half = pl.multiple_of(SHARE + core * WG, WG)
    wgrad = (total_of(own_ref, half, WG) + total_of(other_ref, half, WG)).astype(BF)
    for p in range(N_NEAR):
        send_ref[p, 2 * HALF : 2 * HALF + WG] = wgrad

    def step(g, carry):
        products = []
        for u in range(GROUP):
            t = g * GROUP + u
            slot = slot_ref[0, t]
            product = lax.dot_general(
                tiles_ref[0, t],
                grads[slot >> 3],
                (((0,), (0,)), ((), ())),
                preferred_element_type=F32,
            )
            products.append((slot & 7, jnp.where(t < n, product, 0.0)))
        for col, product in products:
            acc[col] += product
        return carry

    lax.fori_loop(0, (n + GROUP - 1) // GROUP, step, 0)
    for k in range(N_ROW):
        part, place = (k >> 5) * 2 + (k & 1), (k >> 1) & 15
        tile, at = divmod(k * WIN, TILE)
        send_ref[part, place * WIN : (place + 1) * WIN] = acc[tile, at : at + WIN].astype(BF)


def halve_kernel(place_ref, parts_ref, keep_ref, send_ref):
    side = place_ref[1]
    for f in range(N_FAR):
        rows = slice(f * WIN, (f + 1) * WIN)
        z2 = 1 - side if f >> 2 else side
        kept = pl.multiple_of((2 * f + z2) * WIN, WIN)
        sent = pl.multiple_of((2 * f + 1 - z2) * WIN, WIN)
        keep_ref[rows] = total_of(parts_ref, kept, WIN)
        send_ref[rows] = total_of(parts_ref, sent, WIN).astype(BF)
    send_ref[HALF : HALF + WG] = total_of(parts_ref, 2 * HALF, WG).astype(BF)


def deal_kernel(keep_ref, sent_ref, came_ref, send_ref):
    wrows = slice(HALF, HALF + WG)
    wgrad = (sent_ref[wrows].astype(F32) + came_ref[wrows].astype(F32)).astype(BF)
    for f in range(N_FAR):
        rows = slice(f * WIN, (f + 1) * WIN)
        send_ref[f, 0:WIN] = (keep_ref[rows] + came_ref[rows].astype(F32)).astype(BF)
        send_ref[f, WIN : WIN + WG] = wgrad


def last_kernel(parts_ref, win_ref, wgrad_ref):
    win_ref[0] = total_of(parts_ref, 0, WIN).astype(BF)
    wgrad = total_of(parts_ref, WIN, WG).astype(BF)
    for j in range(N_COL):
        wgrad_ref[j] = wgrad


def scale_kernel(scale, wgrad_ref, out_ref):
    out_ref[...] = wgrad_ref[...].astype(F32).reshape(F, F) * scale


def exchange(parts, axes, groups=None):
    return lax.all_to_all(parts, axes, 0, 0, axis_index_groups=groups, tiled=True)


def shape(*dims, dtype=BF):
    return jax.ShapeDtypeStruct(dims, dtype)


def on_device(tiles, tile_slot, tile_count, feats, weight, out_grad):
    swap = [(0, 1), (1, 0)]
    side = lax.axis_index("z2") ^ lax.axis_index("z16")
    place = jnp.stack([lax.axis_index("c"), side]).astype(jnp.int32)
    row_partial = pl.pallas_call(
        forward_kernel,
        out_shape=shape(RT * TILE, F),
        in_specs=[HBM] * 4,
        out_specs=VMEM,
        scratch_shapes=[
            pltpu.SMEM((1, TPD), jnp.int32),
            pltpu.SMEM((1, 1), jnp.int32),
            pltpu.VMEM((TPD, TILE, TILE), BF),
            pltpu.VMEM((CT * TILE, F), BF),
            pltpu.VMEM((RT, TILE, F), F32),
            pltpu.SemaphoreType.DMA((len(FETCHES),)),
            pltpu.SemaphoreType.DMA((3,)),
        ],
        compiler_params=ALL_VMEM,
    )(tile_slot, tile_count, tiles, feats)
    row_parts = exchange(row_partial.reshape(N_COL, SHARE, F), COL)

    activated, grad_send = pl.pallas_call(
        middle_kernel,
        out_shape=(shape(SHARE, F), shape(N_CHIP, SHARE + 2 * WG, F)),
        in_specs=[VMEM] * 3,
        out_specs=(VMEM, VMEM),
        compiler_params=LIMIT,
    )(row_parts, weight, out_grad)
    own_parts = exchange(grad_send, CHIPS)
    other_parts = lax.ppermute(own_parts, "c", swap)

    near_send = pl.pallas_call(
        backward_kernel,
        out_shape=shape(N_NEAR, 2 * HALF + WG, F),
        in_specs=[SMEM] * 3 + [VMEM] * 3,
        out_specs=VMEM,
        scratch_shapes=[
            pltpu.VMEM((RT, TILE, F), BF),
            pltpu.VMEM((CT, TILE, F), F32),
        ],
        compiler_params=LIMIT,
    )(tile_slot, tile_count, place, tiles, own_parts, other_parts)
    near_parts = exchange(near_send, NEAR)

    kept, half_send = pl.pallas_call(
        halve_kernel,
        out_shape=(shape(HALF, F, dtype=F32), shape(HALF + WG, F)),
        in_specs=[SMEM, VMEM],
        out_specs=(VMEM, VMEM),
        compiler_params=LIMIT,
    )(place, near_parts)
    half_came = lax.ppermute(half_send, "z2", swap)

    far_send = pl.pallas_call(
        deal_kernel,
        out_shape=shape(N_FAR, WIN + WG, F),
        in_specs=[VMEM] * 3,
        out_specs=VMEM,
        compiler_params=LIMIT,
    )(kept, half_send, half_came)
    far_parts = exchange(far_send, ROW, FAR_GROUPS)

    window_grad, wgrad_send = pl.pallas_call(
        last_kernel,
        out_shape=(shape(1, WIN, F), shape(N_COL, WG, F)),
        in_specs=[VMEM],
        out_specs=(VMEM, VMEM),
        compiler_params=LIMIT,
    )(far_parts)
    wgrad_parts = exchange(wgrad_send, COL)
    weight_grad = pl.pallas_call(
        functools.partial(scale_kernel, 1.0 / math.sqrt(RT * TILE * N_ROW)),
        out_shape=shape(F, F, dtype=F32),
        in_specs=[VMEM],
        out_specs=VMEM,
        compiler_params=LIMIT,
    )(wgrad_parts)
    return (activated, weight_grad, window_grad)


def solution(mesh):
    fine = Mesh(mesh.devices.reshape((2,) * len(AXES)), AXES)
    placed = (
        P(ROW, COL, None, None),
        P(ROW, COL),
        P(ROW, COL),
        P(COL, None),
        P(),
        P(AXES, None),
    )
    return jax.shard_map(
        on_device,
        mesh=fine,
        in_specs=placed,
        out_specs=(P(AXES, None), P(), P(COL, ROW, None)),
        check_vma=False,
    )
```

```python
import functools
import math

import jax
import jax.numpy as jnp
from jax import lax
from jax.experimental import pallas as pl
from jax.experimental.pallas import tpu as pltpu
from jax.sharding import Mesh
from jax.sharding import PartitionSpec as P

RT, CT, TPD, TILE, F = 4, 8, 24, 256, 256
N_ROW, N_COL = 64, 16
SHARE = RT * TILE // N_COL
WIN = CT * TILE // N_ROW
WG = F // N_COL
WGX = WG // 2

AXES = ("xl", "z16", "z8", "z4", "z2", "z1", "y2", "y1", "xh", "c")
ROW, COL = AXES[:6], AXES[6:]
NEAR = ("xl", "z1")
N_NEAR, N_FAR = 4, 8
FAR_GROUPS = [
    [xl * 32 + f * 4 + (side ^ (f >> 2)) * 2 + z1 for f in range(N_FAR)]
    for xl in range(2)
    for side in range(2)
    for z1 in range(2)
]
HALF = N_FAR * WIN

BF, F32 = jnp.bfloat16, jnp.float32
SMEM = pl.BlockSpec(memory_space=pltpu.SMEM)
VMEM = pl.BlockSpec(memory_space=pltpu.VMEM)
HBM = pl.BlockSpec(memory_space=pltpu.MemorySpace.HBM)
LIMIT = pltpu.CompilerParams(vmem_limit_bytes=16 << 20)
ALL_VMEM = pltpu.CompilerParams(vmem_limit_bytes=59 << 20)


FETCHES = ((0, 4), (4, 12), (12, 24))
GROUP = 8


def forward_kernel(
    slot_hbm, count_hbm, tiles_hbm, feats_hbm, out_ref,
    slot_ref, count_ref, buf, feats, acc, tile_sems, sems,
):
    def tile_copy(g):
        first, end = FETCHES[g]
        rows = pl.ds(first, end - first)
        return pltpu.make_async_copy(tiles_hbm.at[0, rows], buf.at[rows], tile_sems.at[g])

    small = [
        pltpu.make_async_copy(slot_hbm, slot_ref, sems.at[0]),
        pltpu.make_async_copy(count_hbm, count_ref, sems.at[1]),
        pltpu.make_async_copy(feats_hbm, feats, sems.at[2]),
    ]
    for copy in small:
        copy.start()
    for g in range(len(FETCHES)):
        tile_copy(g).start()
    acc[...] = jnp.zeros_like(acc)
    for copy in small:
        copy.wait()
    n = count_ref[0, 0]

    def multiply(first):
        products = []
        for u in range(4):
            t = first + u
            slot = slot_ref[0, t]
            source = feats[pl.ds(pl.multiple_of((slot & 7) * TILE, TILE), TILE), :]
            product = jnp.dot(buf[t], source, preferred_element_type=F32)
            products.append((slot >> 3, jnp.where(t < n, product, 0.0)))
        for row, product in products:
            acc[row] += product

    for g in range(len(FETCHES)):
        tile_copy(g).wait()
        for first in range(*FETCHES[g], 4):

            @pl.when(first < n)
            def _(first=first):
                multiply(first)

    out_ref[...] = acc[...].reshape(RT * TILE, F).astype(BF)


def middle_kernel(parts_ref, weight_ref, out_grad_ref, act_ref, send_ref):
    total = parts_ref[0].astype(F32)
    for j in range(1, N_COL):
        total += parts_ref[j].astype(F32)
    agg = total.astype(BF)
    weight = weight_ref[...]
    pre = jnp.dot(agg, weight, preferred_element_type=F32)
    sig = jax.nn.sigmoid(pre)
    act_ref[...] = (pre * sig).astype(BF)
    grad_pre = (out_grad_ref[...].astype(F32) * sig * (1.0 + pre * (1.0 - sig))).astype(BF)
    share = lax.dot_general(
        grad_pre, weight, (((1,), (1,)), ((), ())), preferred_element_type=F32
    ).astype(BF)
    local = lax.dot_general(
        agg, grad_pre, (((0,), (0,)), ((), ())), preferred_element_type=F32
    ).astype(BF)
    for j in range(N_COL):
        send_ref[j, 0:SHARE] = share
        send_ref[j, SHARE : SHARE + WG] = local[j * WG : (j + 1) * WG]


def total_of(parts_ref, start, size):
    total = parts_ref[0, pl.ds(start, size)].astype(F32)
    for p in range(1, parts_ref.shape[0]):
        total += parts_ref[p, pl.ds(start, size)].astype(F32)
    return total


def backward_kernel(slot_ref, count_ref, tiles_ref, parts_ref, send_ref, grads, acc):
    n, side = count_ref[0, 0], lax.axis_index("z2") ^ lax.axis_index("z16")
    acc[...] = jnp.zeros_like(acc)
    for j in range(N_COL):
        k, at = divmod(j * SHARE, TILE)
        grads[k, at : at + SHARE] = parts_ref[j, 0:SHARE]
    wgrad = total_of(parts_ref, SHARE, WG).astype(BF)
    for p in range(N_NEAR):
        first = p // 2 * WGX
        send_ref[p, 2 * HALF : 2 * HALF + WGX] = wgrad[first : first + WGX]

    def step(g, carry):
        products = []
        for u in range(GROUP):
            t = g * GROUP + u
            slot = slot_ref[0, t]
            product = lax.dot_general(
                tiles_ref[0, t],
                grads[slot >> 3],
                (((0,), (0,)), ((), ())),
                preferred_element_type=F32,
            )
            products.append((slot & 7, jnp.where(t < n, product, 0.0)))
        for col, product in products:
            acc[col] += product
        return carry

    lax.fori_loop(0, (n + GROUP - 1) // GROUP, step, 0)
    for k in range(N_ROW):
        part, f, z2 = (k >> 5) * 2 + (k & 1), (k >> 2) & 7, (k >> 1) & 1
        half = side if z2 == f >> 2 else 1 - side
        place = pl.multiple_of((half * N_FAR + f) * WIN, WIN)
        tile, at = divmod(k * WIN, TILE)
        send_ref[part, pl.ds(place, WIN)] = acc[tile, at : at + WIN].astype(BF)


def halve_kernel(parts_ref, keep_ref, send_ref):
    keep_ref[...] = total_of(parts_ref, 0, HALF)
    send_ref[...] = total_of(parts_ref, HALF, HALF + WGX).astype(BF)


def deal_kernel(keep_ref, sent_ref, came_ref, send_ref):
    wrows = slice(HALF, HALF + WGX)
    wgrad = (sent_ref[wrows].astype(F32) + came_ref[wrows].astype(F32)).astype(BF)
    for f in range(N_FAR):
        rows = slice(f * WIN, (f + 1) * WIN)
        send_ref[f, 0:WIN] = (keep_ref[rows] + came_ref[rows].astype(F32)).astype(BF)
        send_ref[f, WIN : WIN + WGX] = wgrad


def last_kernel(parts_ref, win_ref, wgrad_ref):
    win_ref[0] = total_of(parts_ref, 0, WIN).astype(BF)
    wgrad = total_of(parts_ref, WIN, WGX).astype(BF)
    for p in range(2 * N_COL):
        wgrad_ref[p] = wgrad


def scale_kernel(scale, wgrad_ref, out_ref):
    out_ref[...] = wgrad_ref[...].astype(F32).reshape(F, F) * scale


def exchange(parts, axes, groups=None):
    return lax.all_to_all(parts, axes, 0, 0, axis_index_groups=groups, tiled=True)


def shape(*dims, dtype=BF):
    return jax.ShapeDtypeStruct(dims, dtype)


def on_device(tiles, tile_slot, tile_count, feats, weight, out_grad):
    row_partial = pl.pallas_call(
        forward_kernel,
        out_shape=shape(RT * TILE, F),
        in_specs=[HBM] * 4,
        out_specs=VMEM,
        scratch_shapes=[
            pltpu.SMEM((1, TPD), jnp.int32),
            pltpu.SMEM((1, 1), jnp.int32),
            pltpu.VMEM((TPD, TILE, TILE), BF),
            pltpu.VMEM((CT * TILE, F), BF),
            pltpu.VMEM((RT, TILE, F), F32),
            pltpu.SemaphoreType.DMA((len(FETCHES),)),
            pltpu.SemaphoreType.DMA((3,)),
        ],
        compiler_params=ALL_VMEM,
    )(tile_slot, tile_count, tiles, feats)
    row_parts = exchange(row_partial.reshape(N_COL, SHARE, F), COL)

    activated, grad_send = pl.pallas_call(
        middle_kernel,
        out_shape=(shape(SHARE, F), shape(N_COL, SHARE + WG, F)),
        in_specs=[VMEM] * 3,
        out_specs=(VMEM, VMEM),
        compiler_params=LIMIT,
    )(row_parts, weight, out_grad)
    grad_parts = exchange(grad_send, COL)

    near_send = pl.pallas_call(
        backward_kernel,
        out_shape=shape(N_NEAR, 2 * HALF + WGX, F),
        in_specs=[SMEM] * 2 + [VMEM] * 2,
        out_specs=VMEM,
        scratch_shapes=[
            pltpu.VMEM((RT, TILE, F), BF),
            pltpu.VMEM((CT, TILE, F), F32),
        ],
        compiler_params=LIMIT,
    )(tile_slot, tile_count, tiles, grad_parts)
    near_parts = exchange(near_send, NEAR)

    kept, half_send = pl.pallas_call(
        halve_kernel,
        out_shape=(shape(HALF, F, dtype=F32), shape(HALF + WGX, F)),
        in_specs=[VMEM],
        out_specs=(VMEM, VMEM),
        compiler_params=LIMIT,
    )(near_parts)
    half_came = lax.ppermute(half_send, "z2", [(0, 1), (1, 0)])

    far_send = pl.pallas_call(
        deal_kernel,
        out_shape=shape(N_FAR, WIN + WGX, F),
        in_specs=[VMEM] * 3,
        out_specs=VMEM,
        compiler_params=LIMIT,
    )(kept, half_send, half_came)
    far_parts = exchange(far_send, ROW, FAR_GROUPS)

    window_grad, wgrad_send = pl.pallas_call(
        last_kernel,
        out_shape=(shape(1, WIN, F), shape(2 * N_COL, WGX, F)),
        in_specs=[VMEM],
        out_specs=(VMEM, VMEM),
        compiler_params=LIMIT,
    )(far_parts)
    wgrad_parts = exchange(wgrad_send, COL + ("xl",))
    weight_grad = pl.pallas_call(
        functools.partial(scale_kernel, 1.0 / math.sqrt(RT * TILE * N_ROW)),
        out_shape=shape(F, F, dtype=F32),
        in_specs=[VMEM],
        out_specs=VMEM,
        compiler_params=LIMIT,
    )(wgrad_parts)
    return (activated, weight_grad, window_grad)


def solution(mesh):
    fine = Mesh(mesh.devices.reshape((2,) * len(AXES)), AXES)
    placed = (
        P(ROW, COL, None, None),
        P(ROW, COL),
        P(ROW, COL),
        P(COL, None),
        P(),
        P(AXES, None),
    )
    return jax.shard_map(
        on_device,
        mesh=fine,
        in_specs=placed,
        out_specs=(P(AXES, None), P(), P(COL, ROW, None)),
        check_vma=False,
    )
```

```python
import functools
import math

import jax
import jax.numpy as jnp
from jax import lax
from jax.experimental import pallas as pl
from jax.experimental.pallas import tpu as pltpu
from jax.sharding import Mesh
from jax.sharding import PartitionSpec as P

RT, CT, TPD, TILE, F = 4, 8, 24, 256, 256
N_ROW, N_COL = 64, 16
SHARE = RT * TILE // N_COL
WIN = CT * TILE // N_ROW
WG = F // N_COL
WGZ = WG // 2

AXES = ("xl", "z16", "z8", "z4", "z2", "z1", "y2", "y1", "xh", "c")
ROW, COL = AXES[:6], AXES[6:]
NEAR = ("xl", "z1")
N_NEAR, N_FAR = 4, 8
FAR_GROUPS = [
    [xl * 32 + f * 4 + (side ^ (f >> 2)) * 2 + z1 for f in range(N_FAR)]
    for xl in range(2)
    for side in range(2)
    for z1 in range(2)
]
HALF = N_FAR * WIN

BF, F32 = jnp.bfloat16, jnp.float32
SMEM = pl.BlockSpec(memory_space=pltpu.SMEM)
VMEM = pl.BlockSpec(memory_space=pltpu.VMEM)
HBM = pl.BlockSpec(memory_space=pltpu.MemorySpace.HBM)
LIMIT = pltpu.CompilerParams(vmem_limit_bytes=16 << 20)
ALL_VMEM = pltpu.CompilerParams(vmem_limit_bytes=59 << 20)


FETCHES = ((0, 4), (4, 12), (12, 24))
GROUP = 8


def forward_kernel(
    slot_hbm, count_hbm, tiles_hbm, feats_hbm, out_ref,
    slot_ref, count_ref, buf, feats, acc, tile_sems, sems,
):
    def tile_copy(g):
        first, end = FETCHES[g]
        rows = pl.ds(first, end - first)
        return pltpu.make_async_copy(tiles_hbm.at[0, rows], buf.at[rows], tile_sems.at[g])

    small = [
        pltpu.make_async_copy(slot_hbm, slot_ref, sems.at[0]),
        pltpu.make_async_copy(count_hbm, count_ref, sems.at[1]),
        pltpu.make_async_copy(feats_hbm, feats, sems.at[2]),
    ]
    for copy in small:
        copy.start()
    for g in range(len(FETCHES)):
        tile_copy(g).start()
    acc[...] = jnp.zeros_like(acc)
    for copy in small:
        copy.wait()
    n = count_ref[0, 0]

    def multiply(first):
        products = []
        for u in range(4):
            t = first + u
            slot = slot_ref[0, t]
            source = feats[pl.ds(pl.multiple_of((slot & 7) * TILE, TILE), TILE), :]
            product = jnp.dot(buf[t], source, preferred_element_type=F32)
            products.append((slot >> 3, jnp.where(t < n, product, 0.0)))
        for row, product in products:
            acc[row] += product

    for g in range(len(FETCHES)):
        tile_copy(g).wait()
        for first in range(*FETCHES[g], 4):

            @pl.when(first < n)
            def _(first=first):
                multiply(first)

    out_ref[...] = acc[...].reshape(RT * TILE, F).astype(BF)


def middle_kernel(parts_ref, weight_ref, out_grad_ref, act_ref, send_ref):
    total = parts_ref[0].astype(F32)
    for j in range(1, N_COL):
        total += parts_ref[j].astype(F32)
    agg = total.astype(BF)
    weight = weight_ref[...]
    pre = jnp.dot(agg, weight, preferred_element_type=F32)
    sig = jax.nn.sigmoid(pre)
    act_ref[...] = (pre * sig).astype(BF)
    grad_pre = (out_grad_ref[...].astype(F32) * sig * (1.0 + pre * (1.0 - sig))).astype(BF)
    share = lax.dot_general(
        grad_pre, weight, (((1,), (1,)), ((), ())), preferred_element_type=F32
    ).astype(BF)
    local = lax.dot_general(
        agg, grad_pre, (((0,), (0,)), ((), ())), preferred_element_type=F32
    ).astype(BF)
    for j in range(N_COL):
        send_ref[j, 0:SHARE] = share
        send_ref[j, SHARE : SHARE + WG] = local[j * WG : (j + 1) * WG]


def total_of(parts_ref, start, size):
    total = parts_ref[0, pl.ds(start, size)].astype(F32)
    for p in range(1, parts_ref.shape[0]):
        total += parts_ref[p, pl.ds(start, size)].astype(F32)
    return total


def backward_kernel(
    slot_ref, count_ref, tiles_ref, parts_ref, send_ref, wgrad_ref, grads, acc
):
    n, side = count_ref[0, 0], lax.axis_index("z2") ^ lax.axis_index("z16")
    acc[...] = jnp.zeros_like(acc)
    for j in range(N_COL):
        k, at = divmod(j * SHARE, TILE)
        grads[k, at : at + SHARE] = parts_ref[j, 0:SHARE]
    wgrad_ref[...] = total_of(parts_ref, SHARE, WG)

    def step(g, carry):
        products = []
        for u in range(GROUP):
            t = g * GROUP + u
            slot = slot_ref[0, t]
            product = lax.dot_general(
                tiles_ref[0, t],
                grads[slot >> 3],
                (((0,), (0,)), ((), ())),
                preferred_element_type=F32,
            )
            products.append((slot & 7, jnp.where(t < n, product, 0.0)))
        for col, product in products:
            acc[col] += product
        return carry

    lax.fori_loop(0, (n + GROUP - 1) // GROUP, step, 0)
    for k in range(N_ROW):
        part, f, z2 = (k >> 5) * 2 + (k & 1), (k >> 2) & 7, (k >> 1) & 1
        half = side if z2 == f >> 2 else 1 - side
        place = pl.multiple_of((half * N_FAR + f) * WIN, WIN)
        tile, at = divmod(k * WIN, TILE)
        send_ref[part, pl.ds(place, WIN)] = acc[tile, at : at + WIN].astype(BF)


def halve_kernel(parts_ref, wgrad_ref, keep_ref, send_ref, other_ref):
    low, high = wgrad_ref[0:WGZ], wgrad_ref[WGZ:WG]
    z1 = lax.axis_index("z1")
    own = jnp.where(z1 == 0, low, high).astype(BF)
    keep_ref[0:HALF] = total_of(parts_ref, 0, HALF)
    keep_ref[HALF : HALF + WGZ] = own.astype(F32)
    send_ref[0:HALF] = total_of(parts_ref, HALF, HALF).astype(BF)
    send_ref[HALF : HALF + WGZ] = own
    other_ref[...] = jnp.where(z1 == 0, high, low).astype(BF)


def deal_kernel(keep_ref, came_ref, came_1_ref, came_3_ref, send_ref):
    wrows = slice(HALF, HALF + WGZ)
    near = keep_ref[wrows] + came_1_ref[...].astype(F32)
    next_pair = came_ref[wrows].astype(F32) + came_3_ref[...].astype(F32)
    wgrad = (near + next_pair).astype(BF)
    for f in range(N_FAR):
        rows = slice(f * WIN, (f + 1) * WIN)
        send_ref[f, 0:WIN] = (keep_ref[rows] + came_ref[rows].astype(F32)).astype(BF)
        send_ref[f, WIN : WIN + WGZ] = wgrad


def last_kernel(parts_ref, win_ref, wgrad_ref):
    win_ref[0] = total_of(parts_ref, 0, WIN).astype(BF)
    wgrad = total_of(parts_ref, WIN, WGZ).astype(BF)
    for p in range(4 * N_COL):
        wgrad_ref[p] = wgrad


def scale_kernel(scale, parts_ref, out_ref):
    for q in range(2 * N_COL):
        both = parts_ref[2 * q].astype(F32) + parts_ref[2 * q + 1].astype(F32)
        out_ref[q * WGZ : (q + 1) * WGZ] = both * scale


def exchange(parts, axes, groups=None):
    return lax.all_to_all(parts, axes, 0, 0, axis_index_groups=groups, tiled=True)


def shape(*dims, dtype=BF):
    return jax.ShapeDtypeStruct(dims, dtype)


def on_device(tiles, tile_slot, tile_count, feats, weight, out_grad):
    row_partial = pl.pallas_call(
        forward_kernel,
        out_shape=shape(RT * TILE, F),
        in_specs=[HBM] * 4,
        out_specs=VMEM,
        scratch_shapes=[
            pltpu.SMEM((1, TPD), jnp.int32),
            pltpu.SMEM((1, 1), jnp.int32),
            pltpu.VMEM((TPD, TILE, TILE), BF),
            pltpu.VMEM((CT * TILE, F), BF),
            pltpu.VMEM((RT, TILE, F), F32),
            pltpu.SemaphoreType.DMA((len(FETCHES),)),
            pltpu.SemaphoreType.DMA((3,)),
        ],
        compiler_params=ALL_VMEM,
    )(tile_slot, tile_count, tiles, feats)
    row_parts = exchange(row_partial.reshape(N_COL, SHARE, F), COL)

    activated, grad_send = pl.pallas_call(
        middle_kernel,
        out_shape=(shape(SHARE, F), shape(N_COL, SHARE + WG, F)),
        in_specs=[VMEM] * 3,
        out_specs=(VMEM, VMEM),
        compiler_params=LIMIT,
    )(row_parts, weight, out_grad)
    grad_parts = exchange(grad_send, COL)

    near_send, wgrad = pl.pallas_call(
        backward_kernel,
        out_shape=(shape(N_NEAR, 2 * HALF, F), shape(WG, F, dtype=F32)),
        in_specs=[SMEM] * 2 + [VMEM] * 2,
        out_specs=(VMEM, VMEM),
        scratch_shapes=[
            pltpu.VMEM((RT, TILE, F), BF),
            pltpu.VMEM((CT, TILE, F), F32),
        ],
        compiler_params=LIMIT,
    )(tile_slot, tile_count, tiles, grad_parts)
    near_parts = exchange(near_send, NEAR)

    kept, half_send, other_send = pl.pallas_call(
        halve_kernel,
        out_shape=(
            shape(HALF + WGZ, F, dtype=F32),
            shape(HALF + WGZ, F),
            shape(WGZ, F),
        ),
        in_specs=[VMEM] * 2,
        out_specs=(VMEM,) * 3,
        compiler_params=LIMIT,
    )(near_parts, wgrad)
    half_came = lax.ppermute(half_send, "z2", [(0, 1), (1, 0)])
    other_came_1 = lax.ppermute(other_send, "z1", [(0, 1), (1, 0)])
    other_came_3 = lax.ppermute(other_send, ("z2", "z1"), [(i, i ^ 3) for i in range(4)])

    far_send = pl.pallas_call(
        deal_kernel,
        out_shape=shape(N_FAR, WIN + WGZ, F),
        in_specs=[VMEM] * 4,
        out_specs=VMEM,
        compiler_params=LIMIT,
    )(kept, half_came, other_came_1, other_came_3)
    far_parts = exchange(far_send, ROW, FAR_GROUPS)

    window_grad, wgrad_send = pl.pallas_call(
        last_kernel,
        out_shape=(shape(1, WIN, F), shape(4 * N_COL, WGZ, F)),
        in_specs=[VMEM],
        out_specs=(VMEM, VMEM),
        compiler_params=LIMIT,
    )(far_parts)
    wgrad_parts = exchange(wgrad_send, COL + ("z1", "xl"))
    weight_grad = pl.pallas_call(
        functools.partial(scale_kernel, 1.0 / math.sqrt(RT * TILE * N_ROW)),
        out_shape=shape(F, F, dtype=F32),
        in_specs=[VMEM],
        out_specs=VMEM,
        compiler_params=LIMIT,
    )(wgrad_parts)
    return (activated, weight_grad, window_grad)


def solution(mesh):
    fine = Mesh(mesh.devices.reshape((2,) * len(AXES)), AXES)
    placed = (
        P(ROW, COL, None, None),
        P(ROW, COL),
        P(ROW, COL),
        P(COL, None),
        P(),
        P(AXES, None),
    )
    return jax.shard_map(
        on_device,
        mesh=fine,
        in_specs=placed,
        out_specs=(P(AXES, None), P(), P(COL, ROW, None)),
        check_vma=False,
    )
```

```python
import functools
import math

import jax
import jax.numpy as jnp
from jax import lax
from jax.experimental import pallas as pl
from jax.experimental.pallas import tpu as pltpu
from jax.sharding import Mesh
from jax.sharding import PartitionSpec as P

RT, CT, TPD, TILE, F = 4, 8, 24, 256, 256
N_ROW, N_COL = 64, 16
SHARE = RT * TILE // N_COL
WIN = CT * TILE // N_ROW
WG = F // N_COL
WGX = WG // 2

AXES = ("xl", "z16", "z8", "z4", "z2", "z1", "y2", "y1", "xh", "c")
ROW, COL = AXES[:6], AXES[6:]
NEAR = ("xl", "z1")
N_NEAR, N_FAR = 4, 8
FAR_GROUPS = [
    [xl * 32 + f * 4 + (side ^ (f >> 2)) * 2 + z1 for f in range(N_FAR)]
    for xl in range(2)
    for side in range(2)
    for z1 in range(2)
]
HALF = N_FAR * WIN

BF, F32 = jnp.bfloat16, jnp.float32
SMEM = pl.BlockSpec(memory_space=pltpu.SMEM)
VMEM = pl.BlockSpec(memory_space=pltpu.VMEM)
HBM = pl.BlockSpec(memory_space=pltpu.MemorySpace.HBM)
LIMIT = pltpu.CompilerParams(vmem_limit_bytes=16 << 20)
ALL_VMEM = pltpu.CompilerParams(vmem_limit_bytes=59 << 20)


FETCHES = ((0, 12), (12, 24))
GROUP = 8


def forward_kernel(
    slot_hbm, count_hbm, tiles_hbm, feats_hbm, out_ref,
    slot_ref, count_ref, buf, feats, acc, tile_sems, sems,
):
    def tile_copy(g):
        first, end = FETCHES[g]
        rows = pl.ds(first, end - first)
        return pltpu.make_async_copy(tiles_hbm.at[0, rows], buf.at[rows], tile_sems.at[g])

    small = [
        pltpu.make_async_copy(slot_hbm, slot_ref, sems.at[0]),
        pltpu.make_async_copy(count_hbm, count_ref, sems.at[1]),
        pltpu.make_async_copy(feats_hbm, feats, sems.at[2]),
    ]
    for copy in small:
        copy.start()
    for g in range(len(FETCHES)):
        tile_copy(g).start()
    acc[...] = jnp.zeros_like(acc)
    for copy in small:
        copy.wait()
    n = count_ref[0, 0]

    def multiply(tiles):
        products = []
        for t in tiles:
            slot = slot_ref[0, t]
            source = feats[pl.ds(pl.multiple_of((slot & 7) * TILE, TILE), TILE), :]
            product = jnp.dot(buf[t], source, preferred_element_type=F32)
            products.append((slot >> 3, jnp.where(t < n, product, 0.0)))
        for row, product in products:
            acc[row] += product

    for g in range(len(FETCHES)):
        tile_copy(g).wait()

        @pl.when(FETCHES[g][0] < n)
        def _(g=g):
            for first in range(*FETCHES[g], 4):
                multiply(range(first, first + 4))

    out_ref[...] = acc[...].reshape(RT * TILE, F).astype(BF)


def middle_kernel(parts_ref, weight_ref, out_grad_ref, act_ref, send_ref):
    total = parts_ref[0].astype(F32)
    for j in range(1, N_COL):
        total += parts_ref[j].astype(F32)
    agg = total.astype(BF)
    weight = weight_ref[...]
    pre = jnp.dot(agg, weight, preferred_element_type=F32)
    sig = jax.nn.sigmoid(pre)
    act_ref[...] = (pre * sig).astype(BF)
    grad_pre = (out_grad_ref[...].astype(F32) * sig * (1.0 + pre * (1.0 - sig))).astype(BF)
    share = lax.dot_general(
        grad_pre, weight, (((1,), (1,)), ((), ())), preferred_element_type=F32
    ).astype(BF)
    local = lax.dot_general(
        agg, grad_pre, (((0,), (0,)), ((), ())), preferred_element_type=F32
    ).astype(BF)
    for j in range(N_COL):
        send_ref[j, 0:SHARE] = share
        send_ref[j, SHARE : SHARE + WG] = local[j * WG : (j + 1) * WG]


def total_of(parts_ref, start, size):
    total = parts_ref[0, pl.ds(start, size)].astype(F32)
    for p in range(1, parts_ref.shape[0]):
        total += parts_ref[p, pl.ds(start, size)].astype(F32)
    return total


def backward_kernel(
    slot_ref, count_ref, tiles_ref, parts_ref, send_ref, own_ref, other_ref, grads, acc
):
    n, side = count_ref[0, 0], lax.axis_index("z2") ^ lax.axis_index("z16")
    acc[...] = jnp.zeros_like(acc)
    for j in range(N_COL):
        k, at = divmod(j * SHARE, TILE)
        grads[k, at : at + SHARE] = parts_ref[j, 0:SHARE]
    wgrad = total_of(parts_ref, SHARE, WG)
    low, high, left = wgrad[0:WGX], wgrad[WGX:WG], lax.axis_index("xl") == 0
    own_ref[...] = jnp.where(left, low, high)
    other_ref[...] = jnp.where(left, high, low).astype(BF)

    def step(g, carry):
        products = []
        for u in range(GROUP):
            t = g * GROUP + u
            slot = slot_ref[0, t]
            product = lax.dot_general(
                tiles_ref[0, t],
                grads[slot >> 3],
                (((0,), (0,)), ((), ())),
                preferred_element_type=F32,
            )
            products.append((slot & 7, jnp.where(t < n, product, 0.0)))
        for col, product in products:
            acc[col] += product
        return carry

    lax.fori_loop(0, (n + GROUP - 1) // GROUP, step, 0)
    for k in range(N_ROW):
        part, f, z2 = (k >> 5) * 2 + (k & 1), (k >> 2) & 7, (k >> 1) & 1
        half = side if z2 == f >> 2 else 1 - side
        place = pl.multiple_of((half * N_FAR + f) * WIN, WIN)
        tile, at = divmod(k * WIN, TILE)
        send_ref[part, pl.ds(place, WIN)] = acc[tile, at : at + WIN].astype(BF)


def add_kernel(own_ref, came_ref, out_ref):
    out_ref[...] = (own_ref[...] + came_ref[...].astype(F32)).astype(BF)


def halve_kernel(parts_ref, wgrad_ref, came_ref, keep_ref, send_ref):
    keep_ref[...] = total_of(parts_ref, 0, HALF)
    send_ref[0:HALF] = total_of(parts_ref, HALF, HALF).astype(BF)
    wgrad = wgrad_ref[...].astype(F32) + came_ref[...].astype(F32)
    send_ref[HALF : HALF + WGX] = wgrad.astype(BF)


def deal_kernel(keep_ref, sent_ref, came_ref, send_ref):
    wrows = slice(HALF, HALF + WGX)
    wgrad = (sent_ref[wrows].astype(F32) + came_ref[wrows].astype(F32)).astype(BF)
    for f in range(N_FAR):
        rows = slice(f * WIN, (f + 1) * WIN)
        send_ref[f, 0:WIN] = (keep_ref[rows] + came_ref[rows].astype(F32)).astype(BF)
        send_ref[f, WIN : WIN + WGX] = wgrad


def last_kernel(parts_ref, win_ref, wgrad_ref):
    win_ref[0] = total_of(parts_ref, 0, WIN).astype(BF)
    wgrad = total_of(parts_ref, WIN, WGX).astype(BF)
    for p in range(2 * N_COL):
        wgrad_ref[p] = wgrad


def scale_kernel(scale, wgrad_ref, out_ref):
    out_ref[...] = wgrad_ref[...].astype(F32).reshape(F, F) * scale


def exchange(parts, axes, groups=None):
    return lax.all_to_all(parts, axes, 0, 0, axis_index_groups=groups, tiled=True)


def shape(*dims, dtype=BF):
    return jax.ShapeDtypeStruct(dims, dtype)


def on_device(tiles, tile_slot, tile_count, feats, weight, out_grad):
    row_partial = pl.pallas_call(
        forward_kernel,
        out_shape=shape(RT * TILE, F),
        in_specs=[HBM] * 4,
        out_specs=VMEM,
        scratch_shapes=[
            pltpu.SMEM((1, TPD), jnp.int32),
            pltpu.SMEM((1, 1), jnp.int32),
            pltpu.VMEM((TPD, TILE, TILE), BF),
            pltpu.VMEM((CT * TILE, F), BF),
            pltpu.VMEM((RT, TILE, F), F32),
            pltpu.SemaphoreType.DMA((len(FETCHES),)),
            pltpu.SemaphoreType.DMA((3,)),
        ],
        compiler_params=ALL_VMEM,
    )(tile_slot, tile_count, tiles, feats)
    row_parts = exchange(row_partial.reshape(N_COL, SHARE, F), COL)

    activated, grad_send = pl.pallas_call(
        middle_kernel,
        out_shape=(shape(SHARE, F), shape(N_COL, SHARE + WG, F)),
        in_specs=[VMEM] * 3,
        out_specs=(VMEM, VMEM),
        compiler_params=LIMIT,
    )(row_parts, weight, out_grad)
    grad_parts = exchange(grad_send, COL)

    near_send, wgrad_own, wgrad_other = pl.pallas_call(
        backward_kernel,
        out_shape=(
            shape(N_NEAR, 2 * HALF, F),
            shape(WGX, F, dtype=F32),
            shape(WGX, F),
        ),
        in_specs=[SMEM] * 2 + [VMEM] * 2,
        out_specs=(VMEM,) * 3,
        scratch_shapes=[
            pltpu.VMEM((RT, TILE, F), BF),
            pltpu.VMEM((CT, TILE, F), F32),
        ],
        compiler_params=LIMIT,
    )(tile_slot, tile_count, tiles, grad_parts)
    near_parts = exchange(near_send, NEAR)
    swap = [(0, 1), (1, 0)]
    wgrad_came = lax.ppermute(wgrad_other, "xl", swap)
    wgrad = pl.pallas_call(
        add_kernel,
        out_shape=shape(WGX, F),
        in_specs=[VMEM] * 2,
        out_specs=VMEM,
        compiler_params=LIMIT,
    )(wgrad_own, wgrad_came)
    wgrad_came = lax.ppermute(wgrad, "z1", swap)

    kept, half_send = pl.pallas_call(
        halve_kernel,
        out_shape=(shape(HALF, F, dtype=F32), shape(HALF + WGX, F)),
        in_specs=[VMEM] * 3,
        out_specs=(VMEM, VMEM),
        compiler_params=LIMIT,
    )(near_parts, wgrad, wgrad_came)
    half_came = lax.ppermute(half_send, "z2", swap)

    far_send = pl.pallas_call(
        deal_kernel,
        out_shape=shape(N_FAR, WIN + WGX, F),
        in_specs=[VMEM] * 3,
        out_specs=VMEM,
        compiler_params=LIMIT,
    )(kept, half_send, half_came)
    far_parts = exchange(far_send, ROW, FAR_GROUPS)

    window_grad, wgrad_send = pl.pallas_call(
        last_kernel,
        out_shape=(shape(1, WIN, F), shape(2 * N_COL, WGX, F)),
        in_specs=[VMEM],
        out_specs=(VMEM, VMEM),
        compiler_params=LIMIT,
    )(far_parts)
    wgrad_parts = exchange(wgrad_send, COL + ("xl",))
    weight_grad = pl.pallas_call(
        functools.partial(scale_kernel, 1.0 / math.sqrt(RT * TILE * N_ROW)),
        out_shape=shape(F, F, dtype=F32),
        in_specs=[VMEM],
        out_specs=VMEM,
        compiler_params=LIMIT,
    )(wgrad_parts)
    return (activated, weight_grad, window_grad)


def solution(mesh):
    fine = Mesh(mesh.devices.reshape((2,) * len(AXES)), AXES)
    placed = (
        P(ROW, COL, None, None),
        P(ROW, COL),
        P(ROW, COL),
        P(COL, None),
        P(),
        P(AXES, None),
    )
    return jax.shard_map(
        on_device,
        mesh=fine,
        in_specs=placed,
        out_specs=(P(AXES, None), P(), P(COL, ROW, None)),
        check_vma=False,
    )
```

```python
import functools
import math

import jax
import jax.numpy as jnp
from jax import lax
from jax.experimental import pallas as pl
from jax.experimental.pallas import tpu as pltpu
from jax.sharding import Mesh
from jax.sharding import PartitionSpec as P

RT, CT, TPD, TILE, F = 4, 8, 24, 256, 256
N_ROW, N_COL = 64, 16
SHARE = RT * TILE // N_COL
WIN = CT * TILE // N_ROW
WG = F // N_COL
WGX = WG // 2

AXES = ("xl", "z16", "z8", "z4", "z2", "z1", "y2", "y1", "xh", "c")
ROW, COL = AXES[:6], AXES[6:]
NEAR = ("xl", "z1")
N_NEAR, N_FAR = 4, 8
FAR_GROUPS = [
    [xl * 32 + f * 4 + (side ^ (f >> 2)) * 2 + z1 for f in range(N_FAR)]
    for xl in range(2)
    for side in range(2)
    for z1 in range(2)
]
HALF = N_FAR * WIN

BF, F32 = jnp.bfloat16, jnp.float32
SMEM = pl.BlockSpec(memory_space=pltpu.SMEM)
VMEM = pl.BlockSpec(memory_space=pltpu.VMEM)
HBM = pl.BlockSpec(memory_space=pltpu.MemorySpace.HBM)
LIMIT = pltpu.CompilerParams(vmem_limit_bytes=16 << 20)
ALL_VMEM = pltpu.CompilerParams(vmem_limit_bytes=59 << 20)


FETCHES = ((0, 12), (12, 24))
GROUP = 8


def forward_kernel(
    slot_hbm, count_hbm, tiles_hbm, feats_hbm, out_ref,
    slot_ref, count_ref, buf, feats, acc, tile_sems, sems,
):
    def tile_copy(g):
        first, end = FETCHES[g]
        rows = pl.ds(first, end - first)
        return pltpu.make_async_copy(tiles_hbm.at[0, rows], buf.at[rows], tile_sems.at[g])

    small = [
        pltpu.make_async_copy(slot_hbm, slot_ref, sems.at[0]),
        pltpu.make_async_copy(count_hbm, count_ref, sems.at[1]),
        pltpu.make_async_copy(feats_hbm, feats, sems.at[2]),
    ]
    for copy in small:
        copy.start()
    for g in range(len(FETCHES)):
        tile_copy(g).start()
    acc[...] = jnp.zeros_like(acc)
    for copy in small:
        copy.wait()
    n = count_ref[0, 0]

    def multiply(tiles):
        products = []
        for t in tiles:
            slot = slot_ref[0, t]
            source = feats[pl.ds(pl.multiple_of((slot & 7) * TILE, TILE), TILE), :]
            product = jnp.dot(buf[t], source, preferred_element_type=F32)
            products.append((slot >> 3, jnp.where(t < n, product, 0.0)))
        for row, product in products:
            acc[row] += product

    for g in range(len(FETCHES)):
        tile_copy(g).wait()

        @pl.when(FETCHES[g][0] < n)
        def _(g=g):
            for first in range(*FETCHES[g], 4):
                multiply(range(first, first + 4))

    out_ref[...] = acc[...].reshape(RT * TILE, F).astype(BF)


def middle_kernel(parts_ref, weight_ref, out_grad_ref, act_ref, send_ref):
    total = parts_ref[0].astype(F32)
    for j in range(1, N_COL):
        total += parts_ref[j].astype(F32)
    agg = total.astype(BF)
    weight = weight_ref[...]
    pre = jnp.dot(agg, weight, preferred_element_type=F32)
    sig = jax.nn.sigmoid(pre)
    act_ref[...] = (pre * sig).astype(BF)
    grad_pre = (out_grad_ref[...].astype(F32) * sig * (1.0 + pre * (1.0 - sig))).astype(BF)
    share = lax.dot_general(
        grad_pre, weight, (((1,), (1,)), ((), ())), preferred_element_type=F32
    ).astype(BF)
    local = lax.dot_general(
        agg, grad_pre, (((0,), (0,)), ((), ())), preferred_element_type=F32
    ).astype(BF)
    for j in range(N_COL):
        send_ref[j, 0:SHARE] = share
        send_ref[j, SHARE : SHARE + WG] = local[j * WG : (j + 1) * WG]


def total_of(parts_ref, start, size):
    total = parts_ref[0, pl.ds(start, size)].astype(F32)
    for p in range(1, parts_ref.shape[0]):
        total += parts_ref[p, pl.ds(start, size)].astype(F32)
    return total


def backward_kernel(
    slot_ref, count_ref, tiles_ref, parts_ref, act_ref, send_ref, act_hbm, grads, acc, sem
):
    act_copy = pltpu.make_async_copy(act_ref, act_hbm, sem)
    act_copy.start()
    n, side = count_ref[0, 0], lax.axis_index("z2") ^ lax.axis_index("z16")
    acc[...] = jnp.zeros_like(acc)
    for j in range(N_COL):
        k, at = divmod(j * SHARE, TILE)
        grads[k, at : at + SHARE] = parts_ref[j, 0:SHARE]
    wgrad = total_of(parts_ref, SHARE, WG).astype(BF)
    for p in range(N_NEAR):
        first = p // 2 * WGX
        send_ref[p, 2 * HALF : 2 * HALF + WGX] = wgrad[first : first + WGX]

    def step(g, carry):
        products = []
        for u in range(GROUP):
            t = g * GROUP + u
            slot = slot_ref[0, t]
            product = lax.dot_general(
                tiles_ref[0, t],
                grads[slot >> 3],
                (((0,), (0,)), ((), ())),
                preferred_element_type=F32,
            )
            products.append((slot & 7, jnp.where(t < n, product, 0.0)))
        for col, product in products:
            acc[col] += product
        return carry

    lax.fori_loop(0, (n + GROUP - 1) // GROUP, step, 0)
    for k in range(N_ROW):
        part, f, z2 = (k >> 5) * 2 + (k & 1), (k >> 2) & 7, (k >> 1) & 1
        half = side if z2 == f >> 2 else 1 - side
        place = pl.multiple_of((half * N_FAR + f) * WIN, WIN)
        tile, at = divmod(k * WIN, TILE)
        send_ref[part, pl.ds(place, WIN)] = acc[tile, at : at + WIN].astype(BF)
    act_copy.wait()


def halve_kernel(parts_ref, keep_ref, send_ref):
    keep_ref[...] = total_of(parts_ref, 0, HALF)
    send_ref[...] = total_of(parts_ref, HALF, HALF + WGX).astype(BF)


def deal_kernel(keep_ref, sent_ref, came_ref, send_ref):
    wrows = slice(HALF, HALF + WGX)
    wgrad = (sent_ref[wrows].astype(F32) + came_ref[wrows].astype(F32)).astype(BF)
    for f in range(N_FAR):
        rows = slice(f * WIN, (f + 1) * WIN)
        send_ref[f, 0:WIN] = (keep_ref[rows] + came_ref[rows].astype(F32)).astype(BF)
        send_ref[f, WIN : WIN + WGX] = wgrad


def wgrad_kernel(parts_ref, send_ref):
    wgrad = total_of(parts_ref, WIN, WGX).astype(BF)
    for p in range(2 * N_COL):
        send_ref[p] = wgrad


def last_kernel(scale, parts_ref, wgrad_ref, win_ref, out_ref):
    win_ref[0] = total_of(parts_ref, 0, WIN).astype(BF)
    out_ref[...] = wgrad_ref[...].astype(F32).reshape(F, F) * scale


def exchange(parts, axes, groups=None):
    return lax.all_to_all(parts, axes, 0, 0, axis_index_groups=groups, tiled=True)


def shape(*dims, dtype=BF):
    return jax.ShapeDtypeStruct(dims, dtype)


def on_device(tiles, tile_slot, tile_count, feats, weight, out_grad):
    row_partial = pl.pallas_call(
        forward_kernel,
        out_shape=shape(RT * TILE, F),
        in_specs=[HBM] * 4,
        out_specs=VMEM,
        scratch_shapes=[
            pltpu.SMEM((1, TPD), jnp.int32),
            pltpu.SMEM((1, 1), jnp.int32),
            pltpu.VMEM((TPD, TILE, TILE), BF),
            pltpu.VMEM((CT * TILE, F), BF),
            pltpu.VMEM((RT, TILE, F), F32),
            pltpu.SemaphoreType.DMA((len(FETCHES),)),
            pltpu.SemaphoreType.DMA((3,)),
        ],
        compiler_params=ALL_VMEM,
    )(tile_slot, tile_count, tiles, feats)
    row_parts = exchange(row_partial.reshape(N_COL, SHARE, F), COL)

    activated, grad_send = pl.pallas_call(
        middle_kernel,
        out_shape=(shape(SHARE, F), shape(N_COL, SHARE + WG, F)),
        in_specs=[VMEM] * 3,
        out_specs=(VMEM, VMEM),
        compiler_params=LIMIT,
    )(row_parts, weight, out_grad)
    grad_parts = exchange(grad_send, COL)

    near_send, activated = pl.pallas_call(
        backward_kernel,
        out_shape=(shape(N_NEAR, 2 * HALF + WGX, F), shape(SHARE, F)),
        in_specs=[SMEM] * 2 + [VMEM] * 3,
        out_specs=(VMEM, HBM),
        scratch_shapes=[
            pltpu.VMEM((RT, TILE, F), BF),
            pltpu.VMEM((CT, TILE, F), F32),
            pltpu.SemaphoreType.DMA,
        ],
        compiler_params=LIMIT,
    )(tile_slot, tile_count, tiles, grad_parts, activated)
    near_parts = exchange(near_send, NEAR)

    kept, half_send = pl.pallas_call(
        halve_kernel,
        out_shape=(shape(HALF, F, dtype=F32), shape(HALF + WGX, F)),
        in_specs=[VMEM],
        out_specs=(VMEM, VMEM),
        compiler_params=LIMIT,
    )(near_parts)
    half_came = lax.ppermute(half_send, "z2", [(0, 1), (1, 0)])

    far_send = pl.pallas_call(
        deal_kernel,
        out_shape=shape(N_FAR, WIN + WGX, F),
        in_specs=[VMEM] * 3,
        out_specs=VMEM,
        compiler_params=LIMIT,
    )(kept, half_send, half_came)
    far_parts = exchange(far_send, ROW, FAR_GROUPS)

    wgrad_send = pl.pallas_call(
        wgrad_kernel,
        out_shape=shape(2 * N_COL, WGX, F),
        in_specs=[VMEM],
        out_specs=VMEM,
        compiler_params=LIMIT,
    )(far_parts)
    wgrad_parts = exchange(wgrad_send, COL + ("xl",))
    window_grad, weight_grad = pl.pallas_call(
        functools.partial(last_kernel, 1.0 / math.sqrt(RT * TILE * N_ROW)),
        out_shape=(shape(1, WIN, F), shape(F, F, dtype=F32)),
        in_specs=[VMEM] * 2,
        out_specs=(VMEM, VMEM),
        compiler_params=LIMIT,
    )(far_parts, wgrad_parts)
    return (activated, weight_grad, window_grad)


def solution(mesh):
    fine = Mesh(mesh.devices.reshape((2,) * len(AXES)), AXES)
    placed = (
        P(ROW, COL, None, None),
        P(ROW, COL),
        P(ROW, COL),
        P(COL, None),
        P(),
        P(AXES, None),
    )
    return jax.shard_map(
        on_device,
        mesh=fine,
        in_specs=placed,
        out_specs=(P(AXES, None), P(), P(COL, ROW, None)),
        check_vma=False,
    )
```

```python
import functools
import math

import jax
import jax.numpy as jnp
from jax import lax
from jax.experimental import pallas as pl
from jax.experimental.pallas import tpu as pltpu
from jax.sharding import Mesh
from jax.sharding import PartitionSpec as P

RT, CT, TPD, TILE, F = 4, 8, 24, 256, 256
N_ROW, N_COL = 64, 16
SHARE = RT * TILE // N_COL
WIN = CT * TILE // N_ROW
WG = F // N_COL
WGX = WG // 2

AXES = ("xl", "z16", "z8", "z4", "z2", "z1", "y2", "y1", "xh", "c")
ROW, COL = AXES[:6], AXES[6:]
NEAR = ("xl", "z1")
N_NEAR, N_FAR = 4, 8
FAR_GROUPS = [
    [xl * 32 + f * 4 + (side ^ (f >> 2)) * 2 + z1 for f in range(N_FAR)]
    for xl in range(2)
    for side in range(2)
    for z1 in range(2)
]
HALF = N_FAR * WIN

BF, F32 = jnp.bfloat16, jnp.float32
SMEM = pl.BlockSpec(memory_space=pltpu.SMEM)
VMEM = pl.BlockSpec(memory_space=pltpu.VMEM)
HBM = pl.BlockSpec(memory_space=pltpu.MemorySpace.HBM)
LIMIT = pltpu.CompilerParams(vmem_limit_bytes=16 << 20)
ALL_VMEM = pltpu.CompilerParams(vmem_limit_bytes=59 << 20)


FETCHES = ((0, 12), (12, 24))
GROUP = 8


def forward_kernel(
    slot_hbm, count_hbm, tiles_hbm, feats_hbm, out_ref,
    slot_ref, count_ref, buf, feats, acc, tile_sems, sems,
):
    def tile_copy(g):
        first, end = FETCHES[g]
        rows = pl.ds(first, end - first)
        return pltpu.make_async_copy(tiles_hbm.at[0, rows], buf.at[rows], tile_sems.at[g])

    begun = [
        pltpu.make_async_copy(slot_hbm, slot_ref, sems.at[0]),
        pltpu.make_async_copy(count_hbm, count_ref, sems.at[1]),
        pltpu.make_async_copy(feats_hbm, feats, sems.at[2]),
    ]
    for copy in begun:
        copy.start()
    for g in range(len(FETCHES)):
        tile_copy(g).start()
    acc[...] = jnp.zeros_like(acc)
    for copy in begun:
        copy.wait()
    n = count_ref[0, 0]

    def multiply(tiles):
        products = []
        for t in tiles:
            slot = slot_ref[0, t]
            source = feats[pl.ds(pl.multiple_of((slot & 7) * TILE, TILE), TILE), :]
            product = jnp.dot(buf[t], source, preferred_element_type=F32)
            products.append((slot >> 3, jnp.where(t < n, product, 0.0)))
        for row, product in products:
            acc[row] += product

    for g in range(len(FETCHES)):
        tile_copy(g).wait()

        @pl.when(FETCHES[g][0] < n)
        def _(g=g):
            for first in range(*FETCHES[g], 4):
                multiply(range(first, first + 4))

    out_ref[...] = acc[...].reshape(RT * TILE, F).astype(BF)


def middle_kernel(parts_ref, weight_ref, out_grad_ref, act_ref, send_ref):
    total = parts_ref[0].astype(F32)
    for j in range(1, N_COL):
        total += parts_ref[j].astype(F32)
    agg = total.astype(BF)
    weight = weight_ref[...]
    pre = jnp.dot(agg, weight, preferred_element_type=F32)
    sig = jax.nn.sigmoid(pre)
    act_ref[...] = (pre * sig).astype(BF)
    grad_pre = (out_grad_ref[...].astype(F32) * sig * (1.0 + pre * (1.0 - sig))).astype(BF)
    share = lax.dot_general(
        grad_pre, weight, (((1,), (1,)), ((), ())), preferred_element_type=F32
    ).astype(BF)
    local = lax.dot_general(
        agg, grad_pre, (((0,), (0,)), ((), ())), preferred_element_type=F32
    ).astype(BF)
    for j in range(N_COL):
        send_ref[j, 0:SHARE] = share
        send_ref[j, SHARE : SHARE + WG] = local[j * WG : (j + 1) * WG]


def total_of(parts_ref, start, size):
    total = parts_ref[0, pl.ds(start, size)].astype(F32)
    for p in range(1, parts_ref.shape[0]):
        total += parts_ref[p, pl.ds(start, size)].astype(F32)
    return total


def backward_kernel(
    slot_ref, count_ref, tiles_ref, parts_ref, act_ref, send_ref, act_hbm, grads, acc, sem
):
    act_copy = pltpu.make_async_copy(act_ref, act_hbm, sem)
    act_copy.start()
    n, side = count_ref[0, 0], lax.axis_index("z2") ^ lax.axis_index("z16")
    acc[...] = jnp.zeros_like(acc)
    for j in range(N_COL):
        k, at = divmod(j * SHARE, TILE)
        grads[k, at : at + SHARE] = parts_ref[j, 0:SHARE]
    wgrad = total_of(parts_ref, SHARE, WG).astype(BF)
    for p in range(N_NEAR):
        first = p // 2 * WGX
        send_ref[p, 2 * HALF : 2 * HALF + WGX] = wgrad[first : first + WGX]

    def step(g, carry):
        products = []
        for u in range(GROUP):
            t = g * GROUP + u
            slot = slot_ref[0, t]
            product = lax.dot_general(
                tiles_ref[0, t],
                grads[slot >> 3],
                (((0,), (0,)), ((), ())),
                preferred_element_type=F32,
            )
            products.append((slot & 7, jnp.where(t < n, product, 0.0)))
        for col, product in products:
            acc[col] += product
        return carry

    lax.fori_loop(0, (n + GROUP - 1) // GROUP, step, 0)
    for k in range(N_ROW):
        part, f, z2 = (k >> 5) * 2 + (k & 1), (k >> 2) & 7, (k >> 1) & 1
        half = side if z2 == f >> 2 else 1 - side
        place = pl.multiple_of((half * N_FAR + f) * WIN, WIN)
        tile, at = divmod(k * WIN, TILE)
        send_ref[part, pl.ds(place, WIN)] = acc[tile, at : at + WIN].astype(BF)
    act_copy.wait()


def halve_kernel(parts_ref, keep_ref, send_ref):
    keep_ref[...] = total_of(parts_ref, 0, HALF)
    send_ref[...] = total_of(parts_ref, HALF, HALF + WGX).astype(BF)


def deal_kernel(keep_ref, sent_ref, came_ref, send_ref):
    wrows = slice(HALF, HALF + WGX)
    wgrad = (sent_ref[wrows].astype(F32) + came_ref[wrows].astype(F32)).astype(BF)
    for f in range(N_FAR):
        rows = slice(f * WIN, (f + 1) * WIN)
        send_ref[f, 0:WIN] = (keep_ref[rows] + came_ref[rows].astype(F32)).astype(BF)
        send_ref[f, WIN : WIN + WGX] = wgrad


def wgrad_kernel(parts_ref, send_ref):
    wgrad = total_of(parts_ref, WIN, WGX).astype(BF)
    for p in range(2 * N_COL):
        send_ref[p] = wgrad


def last_kernel(scale, parts_ref, wgrad_ref, win_ref, out_ref):
    win_ref[0] = total_of(parts_ref, 0, WIN).astype(BF)
    out_ref[...] = wgrad_ref[...].astype(F32).reshape(F, F) * scale


def exchange(parts, axes, groups=None):
    return lax.all_to_all(parts, axes, 0, 0, axis_index_groups=groups, tiled=True)


def shape(*dims, dtype=BF):
    return jax.ShapeDtypeStruct(dims, dtype)


def on_device(tiles, tile_slot, tile_count, feats, weight, out_grad):
    row_partial = pl.pallas_call(
        forward_kernel,
        out_shape=shape(RT * TILE, F),
        in_specs=[HBM] * 4,
        out_specs=VMEM,
        scratch_shapes=[
            pltpu.SMEM((1, TPD), jnp.int32),
            pltpu.SMEM((1, 1), jnp.int32),
            pltpu.VMEM((TPD, TILE, TILE), BF),
            pltpu.VMEM((CT * TILE, F), BF),
            pltpu.VMEM((RT, TILE, F), F32),
            pltpu.SemaphoreType.DMA((len(FETCHES),)),
            pltpu.SemaphoreType.DMA((3,)),
        ],
        compiler_params=ALL_VMEM,
    )(tile_slot, tile_count, tiles, feats)
    row_parts = exchange(row_partial.reshape(N_COL, SHARE, F), COL)

    activated, grad_send = pl.pallas_call(
        middle_kernel,
        out_shape=(shape(SHARE, F), shape(N_COL, SHARE + WG, F)),
        in_specs=[VMEM] * 3,
        out_specs=(VMEM, VMEM),
        compiler_params=LIMIT,
    )(row_parts, weight, out_grad)
    grad_parts = exchange(grad_send, COL)

    near_send, activated = pl.pallas_call(
        backward_kernel,
        out_shape=(shape(N_NEAR, 2 * HALF + WGX, F), shape(SHARE, F)),
        in_specs=[SMEM] * 2 + [VMEM] * 3,
        out_specs=(VMEM, HBM),
        scratch_shapes=[
            pltpu.VMEM((RT, TILE, F), BF),
            pltpu.VMEM((CT, TILE, F), F32),
            pltpu.SemaphoreType.DMA,
        ],
        compiler_params=LIMIT,
    )(tile_slot, tile_count, tiles, grad_parts, activated)
    near_parts = exchange(near_send, NEAR)

    kept, half_send = pl.pallas_call(
        halve_kernel,
        out_shape=(shape(HALF, F, dtype=F32), shape(HALF + WGX, F)),
        in_specs=[VMEM],
        out_specs=(VMEM, VMEM),
        compiler_params=LIMIT,
    )(near_parts)
    half_came = lax.ppermute(half_send, "z2", [(0, 1), (1, 0)])

    far_send = pl.pallas_call(
        deal_kernel,
        out_shape=shape(N_FAR, WIN + WGX, F),
        in_specs=[VMEM] * 3,
        out_specs=VMEM,
        compiler_params=LIMIT,
    )(kept, half_send, half_came)
    far_parts = exchange(far_send, ROW, FAR_GROUPS)

    wgrad_send = pl.pallas_call(
        wgrad_kernel,
        out_shape=shape(2 * N_COL, WGX, F),
        in_specs=[VMEM],
        out_specs=VMEM,
        compiler_params=LIMIT,
    )(far_parts)
    wgrad_parts = exchange(wgrad_send, COL + ("xl",))
    window_grad, weight_grad = pl.pallas_call(
        functools.partial(last_kernel, 1.0 / math.sqrt(RT * TILE * N_ROW)),
        out_shape=(shape(1, WIN, F), shape(F, F, dtype=F32)),
        in_specs=[VMEM] * 2,
        out_specs=(VMEM, VMEM),
        compiler_params=LIMIT,
    )(far_parts, wgrad_parts)
    return (activated, weight_grad, window_grad)


def solution(mesh):
    fine = Mesh(mesh.devices.reshape((2,) * len(AXES)), AXES)
    placed = (
        P(ROW, COL, None, None),
        P(ROW, COL),
        P(ROW, COL),
        P(COL, None),
        P(),
        P(AXES, None),
    )
    return jax.shard_map(
        on_device,
        mesh=fine,
        in_specs=placed,
        out_specs=(P(AXES, None), P(), P(COL, ROW, None)),
        check_vma=False,
    )
```

```python
import functools
import math

import jax
import jax.numpy as jnp
from jax import lax
from jax.experimental import pallas as pl
from jax.experimental.pallas import tpu as pltpu
from jax.sharding import Mesh
from jax.sharding import PartitionSpec as P

RT, CT, TPD, TILE, F = 4, 8, 24, 256, 256
N_ROW, N_COL = 64, 16
SHARE = RT * TILE // N_COL
WIN = CT * TILE // N_ROW
WG = F // N_COL
WGX = WG // 2

AXES = ("xl", "z16", "z8", "z4", "z2", "z1", "y2", "y1", "xh", "c")
ROW, COL = AXES[:6], AXES[6:]
NEAR = ("xl", "z1")
N_NEAR, N_FAR = 4, 8
FAR_GROUPS = [
    [xl * 32 + f * 4 + (side ^ (f >> 2)) * 2 + z1 for f in range(N_FAR)]
    for xl in range(2)
    for side in range(2)
    for z1 in range(2)
]
HALF = N_FAR * WIN

BF, F32 = jnp.bfloat16, jnp.float32
SMEM = pl.BlockSpec(memory_space=pltpu.SMEM)
VMEM = pl.BlockSpec(memory_space=pltpu.VMEM)
HBM = pl.BlockSpec(memory_space=pltpu.MemorySpace.HBM)
LIMIT = pltpu.CompilerParams(vmem_limit_bytes=16 << 20)
ALL_VMEM = pltpu.CompilerParams(vmem_limit_bytes=59 << 20)


FETCHES = ((0, 12), (12, 24))
GROUP = 8


def forward_kernel(
    slot_hbm, count_hbm, tiles_hbm, feats_hbm, out_ref,
    slot_ref, count_ref, buf, feats, acc, tile_sems, sems,
):
    def tile_copy(g):
        first, end = FETCHES[g]
        rows = pl.ds(first, end - first)
        return pltpu.make_async_copy(tiles_hbm.at[0, rows], buf.at[rows], tile_sems.at[g])

    begun = [
        pltpu.make_async_copy(slot_hbm, slot_ref, sems.at[0]),
        pltpu.make_async_copy(count_hbm, count_ref, sems.at[1]),
        pltpu.make_async_copy(feats_hbm, feats, sems.at[2]),
    ]
    for copy in begun:
        copy.start()
    for g in range(len(FETCHES)):
        tile_copy(g).start()
    acc[...] = jnp.zeros_like(acc)
    for copy in begun:
        copy.wait()
    n = count_ref[0, 0]

    def multiply(tiles):
        products = []
        for t in tiles:
            slot = slot_ref[0, t]
            source = feats[pl.ds(pl.multiple_of((slot & 7) * TILE, TILE), TILE), :]
            product = jnp.dot(buf[t], source, preferred_element_type=F32)
            products.append((slot >> 3, jnp.where(t < n, product, 0.0)))
        for row, product in products:
            acc[row] += product

    for g in range(len(FETCHES)):
        tile_copy(g).wait()

        @pl.when(FETCHES[g][0] < n)
        def _(g=g):
            for first in range(*FETCHES[g], 4):
                multiply(range(first, first + 4))

    out_ref[...] = acc[...].reshape(RT * TILE, F).astype(BF)


def middle_kernel(parts_ref, weight_ref, out_grad_ref, act_ref, send_ref):
    total = parts_ref[0].astype(F32)
    for j in range(1, N_COL):
        total += parts_ref[j].astype(F32)
    agg = total.astype(BF)
    weight = weight_ref[...]
    pre = jnp.dot(agg, weight, preferred_element_type=F32)
    sig = jax.nn.sigmoid(pre)
    act_ref[...] = (pre * sig).astype(BF)
    grad_pre = (out_grad_ref[...].astype(F32) * sig * (1.0 + pre * (1.0 - sig))).astype(BF)
    share = lax.dot_general(
        grad_pre, weight, (((1,), (1,)), ((), ())), preferred_element_type=F32
    ).astype(BF)
    local = lax.dot_general(
        agg, grad_pre, (((0,), (0,)), ((), ())), preferred_element_type=F32
    ).astype(BF)
    for j in range(N_COL):
        send_ref[j, 0:SHARE] = share
        send_ref[j, SHARE : SHARE + WG] = local[j * WG : (j + 1) * WG]


def total_of(parts_ref, start, size):
    total = parts_ref[0, pl.ds(start, size)].astype(F32)
    for p in range(1, parts_ref.shape[0]):
        total += parts_ref[p, pl.ds(start, size)].astype(F32)
    return total


def backward_kernel(
    slot_ref, count_ref, tiles_ref, parts_ref, act_ref, send_ref, act_hbm, grads, acc, sem
):
    act_copy = pltpu.make_async_copy(act_ref, act_hbm, sem)
    act_copy.start()
    n, side = count_ref[0, 0], lax.axis_index("z2") ^ lax.axis_index("z16")
    acc[...] = jnp.zeros_like(acc)
    for j in range(N_COL):
        k, at = divmod(j * SHARE, TILE)
        grads[k, at : at + SHARE] = parts_ref[j, 0:SHARE]
    wgrad = total_of(parts_ref, SHARE, WG).astype(BF)
    for p in range(N_NEAR):
        first = p // 2 * WGX
        send_ref[p, 2 * HALF : 2 * HALF + WGX] = wgrad[first : first + WGX]

    def step(g, carry):
        products = []
        for u in range(GROUP):
            t = g * GROUP + u
            slot = slot_ref[0, t]
            product = lax.dot_general(
                tiles_ref[0, t],
                grads[slot >> 3],
                (((0,), (0,)), ((), ())),
                preferred_element_type=F32,
            )
            products.append((slot & 7, jnp.where(t < n, product, 0.0)))
        for col, product in products:
            acc[col] += product
        return carry

    lax.fori_loop(0, (n + GROUP - 1) // GROUP, step, 0)
    for k in range(N_ROW):
        part, f, z2 = (k >> 5) * 2 + (k & 1), (k >> 2) & 7, (k >> 1) & 1
        half = side if z2 == f >> 2 else 1 - side
        place = pl.multiple_of((half * N_FAR + f) * WIN, WIN)
        tile, at = divmod(k * WIN, TILE)
        send_ref[part, pl.ds(place, WIN)] = acc[tile, at : at + WIN].astype(BF)
    act_copy.wait()


def send_kernel(parts_ref, send_ref):
    send_ref[...] = total_of(parts_ref, HALF, HALF + WGX).astype(BF)


def keep_kernel(parts_ref, keep_ref):
    keep_ref[...] = total_of(parts_ref, 0, HALF)


def deal_kernel(keep_ref, sent_ref, came_ref, send_ref):
    wrows = slice(HALF, HALF + WGX)
    wgrad = (sent_ref[wrows].astype(F32) + came_ref[wrows].astype(F32)).astype(BF)
    for f in range(N_FAR):
        rows = slice(f * WIN, (f + 1) * WIN)
        send_ref[f, 0:WIN] = (keep_ref[rows] + came_ref[rows].astype(F32)).astype(BF)
        send_ref[f, WIN : WIN + WGX] = wgrad


def wgrad_kernel(parts_ref, send_ref):
    wgrad = total_of(parts_ref, WIN, WGX).astype(BF)
    for p in range(2 * N_COL):
        send_ref[p] = wgrad


def last_kernel(scale, parts_ref, wgrad_ref, win_ref, out_ref):
    win_ref[0] = total_of(parts_ref, 0, WIN).astype(BF)
    out_ref[...] = wgrad_ref[...].astype(F32).reshape(F, F) * scale


def exchange(parts, axes, groups=None):
    return lax.all_to_all(parts, axes, 0, 0, axis_index_groups=groups, tiled=True)


def shape(*dims, dtype=BF):
    return jax.ShapeDtypeStruct(dims, dtype)


def on_device(tiles, tile_slot, tile_count, feats, weight, out_grad):
    row_partial = pl.pallas_call(
        forward_kernel,
        out_shape=shape(RT * TILE, F),
        in_specs=[HBM] * 4,
        out_specs=VMEM,
        scratch_shapes=[
            pltpu.SMEM((1, TPD), jnp.int32),
            pltpu.SMEM((1, 1), jnp.int32),
            pltpu.VMEM((TPD, TILE, TILE), BF),
            pltpu.VMEM((CT * TILE, F), BF),
            pltpu.VMEM((RT, TILE, F), F32),
            pltpu.SemaphoreType.DMA((len(FETCHES),)),
            pltpu.SemaphoreType.DMA((3,)),
        ],
        compiler_params=ALL_VMEM,
    )(tile_slot, tile_count, tiles, feats)
    row_parts = exchange(row_partial.reshape(N_COL, SHARE, F), COL)

    activated, grad_send = pl.pallas_call(
        middle_kernel,
        out_shape=(shape(SHARE, F), shape(N_COL, SHARE + WG, F)),
        in_specs=[VMEM] * 3,
        out_specs=(VMEM, VMEM),
        compiler_params=LIMIT,
    )(row_parts, weight, out_grad)
    grad_parts = exchange(grad_send, COL)

    near_send, activated = pl.pallas_call(
        backward_kernel,
        out_shape=(shape(N_NEAR, 2 * HALF + WGX, F), shape(SHARE, F)),
        in_specs=[SMEM] * 2 + [VMEM] * 3,
        out_specs=(VMEM, HBM),
        scratch_shapes=[
            pltpu.VMEM((RT, TILE, F), BF),
            pltpu.VMEM((CT, TILE, F), F32),
            pltpu.SemaphoreType.DMA,
        ],
        compiler_params=LIMIT,
    )(tile_slot, tile_count, tiles, grad_parts, activated)
    near_parts = exchange(near_send, NEAR)

    half_send = pl.pallas_call(
        send_kernel,
        out_shape=shape(HALF + WGX, F),
        in_specs=[VMEM],
        out_specs=VMEM,
        compiler_params=LIMIT,
    )(near_parts)
    half_came = lax.ppermute(half_send, "z2", [(0, 1), (1, 0)])
    kept = pl.pallas_call(
        keep_kernel,
        out_shape=shape(HALF, F, dtype=F32),
        in_specs=[VMEM],
        out_specs=VMEM,
        compiler_params=LIMIT,
    )(near_parts)

    far_send = pl.pallas_call(
        deal_kernel,
        out_shape=shape(N_FAR, WIN + WGX, F),
        in_specs=[VMEM] * 3,
        out_specs=VMEM,
        compiler_params=LIMIT,
    )(kept, half_send, half_came)
    far_parts = exchange(far_send, ROW, FAR_GROUPS)

    wgrad_send = pl.pallas_call(
        wgrad_kernel,
        out_shape=shape(2 * N_COL, WGX, F),
        in_specs=[VMEM],
        out_specs=VMEM,
        compiler_params=LIMIT,
    )(far_parts)
    wgrad_parts = exchange(wgrad_send, COL + ("xl",))
    window_grad, weight_grad = pl.pallas_call(
        functools.partial(last_kernel, 1.0 / math.sqrt(RT * TILE * N_ROW)),
        out_shape=(shape(1, WIN, F), shape(F, F, dtype=F32)),
        in_specs=[VMEM] * 2,
        out_specs=(VMEM, VMEM),
        compiler_params=LIMIT,
    )(far_parts, wgrad_parts)
    return (activated, weight_grad, window_grad)


def solution(mesh):
    fine = Mesh(mesh.devices.reshape((2,) * len(AXES)), AXES)
    placed = (
        P(ROW, COL, None, None),
        P(ROW, COL),
        P(ROW, COL),
        P(COL, None),
        P(),
        P(AXES, None),
    )
    return jax.shard_map(
        on_device,
        mesh=fine,
        in_specs=placed,
        out_specs=(P(AXES, None), P(), P(COL, ROW, None)),
        check_vma=False,
    )
```
